32 devices in a mesh: tm: 8 (over z, y), ep: 4 (over x, core).
Axes of the slice: x: 2, y: 2, z: 4, core: 2. Of those that a mesh axis runs over, the one named last changes fastest.
Arguments:
- queries: bfloat16 [4096, 1024], P(('tm', 'ep')), may hold values from -256 to 256
- keys: bfloat16 [4096, 1024], P(('tm', 'ep')), may hold values from -6 to 6
- values: bfloat16 [4096, 1024], P(('tm', 'ep')), may hold values from -6 to 6
- stream: bfloat16 [4096, 1024], P(('tm', 'ep')), may hold values from -16 to 16
- grad_out: bfloat16 [4096, 1024], P(('tm', 'ep')), may hold values from -6 to 6
- norm_gain: float32 [1024], replicated, may hold values from 0.1 to 1.9
- gate_probs: float32 [4096, 2], P(('tm', 'ep')), may hold values from 0.1 to 0.9
- routes: int32 [4096, 2], P(('tm', 'ep')), may hold values from 0 to 7, all different within a row; in each aligned block of 128 rows (0 to 127, 128 to 255, ...) at most 48 rows name the same one
- w_gate: bfloat16 [8, 1024, 4096], P('tm', None, 'ep'), may hold values from -0.1875 to 0.1875
- w_up: bfloat16 [8, 1024, 4096], P('tm', None, 'ep'), may hold values from -0.1875 to 0.1875
- w_down: bfloat16 [8, 4096, 1024], P('tm', 'ep'), may hold values from -0.09375 to 0.09375
Outputs:
- queries_grad: bfloat16 [4096, 1024], P(('tm', 'ep'))
- keys_grad: bfloat16 [4096, 1024], P(('tm', 'ep'))
- values_grad: bfloat16 [4096, 1024], P(('tm', 'ep'))
- stream_grad: bfloat16 [4096, 1024], P(('tm', 'ep'))
- gate_weight_grad: float32 [8, 1024, 4096], P('tm', None, 'ep')
- up_weight_grad: float32 [8, 1024, 4096], P('tm', None, 'ep')
- down_weight_grad: float32 [8, 4096, 1024], P('tm', 'ep')
The draws below stay inside these ranges and needn't reach their ends.
Inputs may be any that keep to these rules, and one draw needn't show every extreme that they name: `routes`: in the frames of one device no expert is named by more than 48 frames, a bound that some block reaches.
All inputs are finite; a program needn't handle non-finite values.
Results may differ from the reference program's by a relative error of at most 0.015.
Values may be sent and summed in bfloat16 or wider, within the bound.
A program may use at most 128 MiB of HBM per device.

```python
import math
import jax
import jax.numpy as jnp
import numpy as np
from jax import lax

D = 1024
HEADS = 16
HEAD = 64
HID = 4096
TOPK = 2
SPAN = 64
LEFT = 256
FR_DEV = 128
EXPERTS = 8
FRAMES = 4096
CAP = 48
N_TM = 8
N_EP = 4


def attention_pair(key):
    base_key = jax.random.fold_in(key, 4711)
    keys_base = jnp.clip(jax.random.normal(jax.random.fold_in(base_key, 1), (FRAMES, D), jnp.float32), -6.0, 6.0)
    queries_base = jnp.clip(jax.random.normal(jax.random.fold_in(base_key, 2), (FRAMES, D), jnp.float32), -6.0, 6.0)
    return (queries_base, keys_base)


def draw_queries(key, part):
    query_out, key_out = attention_pair(key)
    return query_out.astype(jnp.bfloat16)


def draw_keys(key, part):
    query_out, key_out = attention_pair(key)
    return key_out.astype(jnp.bfloat16)


def draw_stream(key, part):
    base_key = jax.random.fold_in(key, 913)
    column_scale = jnp.exp(jax.random.uniform(jax.random.fold_in(base_key, 1), (1, D), minval=math.log(0.3), maxval=math.log(3.0)))
    row_scale = jnp.exp(jax.random.uniform(jax.random.fold_in(base_key, 2), (FRAMES, 1), minval=math.log(0.1), maxval=math.log(1.0)))
    core_vals = jnp.clip(jax.random.normal(jax.random.fold_in(base_key, 4), (FRAMES, D), jnp.float32), -5.0, 5.0)
    return (core_vals * row_scale * column_scale).astype(jnp.bfloat16)


def steps_of(own_key, dims, shards, smallest, high):
    gain, own = 1.0, jax.random.fold_in(own_key, 6)
    for position, shards_of in shards:
        steps = jnp.exp(jax.random.uniform(jax.random.fold_in(own, position), (shards_of,), jnp.float32, smallest / len(shards), high / len(shards)))
        gain = gain * jnp.repeat(steps, dims[position] // shards_of).reshape([-1 if axis == position else 1 for axis in range(len(dims))])
    return gain


def routed_block(stream_key, own, number, rows, count, top, reach, skew):
    ranking = jax.random.permutation(stream_key, count)
    packed, ordinary = shares(count, rows * top, reach, skew, True), shares(count, rows * top, reach, skew, False)
    places = jnp.arange(count)

    def named(sizes, turn):
        used = int((sizes > 0).sum())
        fixed = max(1, used // 4)
        passed = fixed + (places - fixed + turn * (used - fixed)) % max(1, count - fixed)
        return jnp.zeros((count,), jnp.int32).at[ranking[jnp.where(places < fixed, places, passed)]].set(jnp.asarray(sizes, jnp.int32))

    sizes = jnp.where(number % 4 == 0, named(packed, number // 4), named(ordinary, number - number // 4 - 1))
    mixed = jax.random.permutation(jax.random.fold_in(own, 3), count)
    source_of, sink = mixed[0:count // 2 * 2:2], mixed[1:count // 2 * 2:2]
    room = jnp.minimum(sizes[source_of] - 1, reach - sizes[sink]) // 2
    room = jnp.where((source_of == ranking[0]) | (sink == ranking[0]) | (sizes[sink] == 0), 0, jnp.maximum(room, 0))
    passed = jax.random.randint(jax.random.fold_in(own, 4), (count // 2,), 0, 1 << 20) % (room + 1)
    sizes = sizes.at[source_of].add(-passed).at[sink].add(passed)
    items = jnp.searchsorted(jnp.cumsum(sizes), jnp.arange(rows * top), side="right").astype(jnp.int32)
    listing = items.reshape(top, rows).T
    listing = listing[jax.random.permutation(jax.random.fold_in(own, 1), rows)]
    turn = jax.random.randint(jax.random.fold_in(own, 2), (rows, 1), 0, top)
    return jnp.take_along_axis(listing, (jnp.arange(top)[None, :] + turn) % top, axis=1)


def shares(number_of, total, bound, skew, full):
    loads = [(1 << 20) // math.isqrt(grade ** skew) + 1 for grade in range(1, number_of + 1)]
    largest = bound if full else min(bound, max(-(-total // number_of), total * loads[0] // sum(loads)))
    least = 1 if total - largest >= number_of - 1 else 0
    counts, spare = [largest] + [least] * (number_of - 1), total - largest - least * (number_of - 1)
    while spare > 0:
        free = [i for i in range(1, number_of) if counts[i] < largest] or [i for i in range(1, number_of) if counts[i] < bound]
        whole, remaining = sum([loads[i] for i in free]), spare
        for i in free:
            addition = min(bound - counts[i], max(1, remaining * loads[i] // whole), spare)
            counts[i] = counts[i] + addition
            spare = spare - addition
    return np.array(counts)


def scatter_about(own_key, extent, scale, bound, cuts=(), kind=jnp.bfloat16):
    drawn = scale * jax.random.normal(own_key, extent, jnp.float32)
    if cuts:
        drawn = drawn * steps_of(own_key, extent, cuts, -0.22, 0.18)
    return jnp.clip(drawn, -bound, bound).astype(kind)


def setup_inputs(seed: int = 0) -> dict:
    streams_of = jax.random.split(jax.random.key(seed), 12)
    queries = draw_queries(jax.random.fold_in(streams_of[11], 71), 0)
    keys = draw_keys(jax.random.fold_in(streams_of[11], 71), 0)
    values = scatter_about(streams_of[2], (FRAMES, D), 1.0, 6.0, ((0, 32),))
    stream = draw_stream(jax.random.fold_in(streams_of[11], 71), 0)
    grad_out = scatter_about(streams_of[4], (FRAMES, D), 1.0, 6.0, ((0, 32),))
    norm_gain = jnp.clip(1.0 + 0.18 * jax.random.normal(streams_of[5], (D,), jnp.float32), 0.1, 1.9)
    gate_probs = jnp.clip(0.1 + 0.79999997 * jax.random.uniform(streams_of[6], (FRAMES, TOPK), jnp.float32) ** steps_of(streams_of[6], (FRAMES, TOPK), ((0, 32),), -0.2, 0.2), 0.1, 0.9)
    routes_keys = jax.random.split(jax.random.fold_in(streams_of[7], 1), FRAMES // FR_DEV)
    routes_turns = jax.random.permutation(jax.random.fold_in(streams_of[7], 3), FRAMES // FR_DEV)
    routes = jax.vmap(lambda own, number: routed_block(jax.random.fold_in(streams_of[7], 2), own, number, FR_DEV, EXPERTS, TOPK, CAP, 2))(routes_keys, routes_turns).reshape((FRAMES, TOPK))
    w_gate = scatter_about(streams_of[8], (EXPERTS, D, HID), D ** -0.5, 0.1875, ((0, 8), (2, 4)))
    w_up = scatter_about(streams_of[9], (EXPERTS, D, HID), D ** -0.5, 0.1875, ((0, 8), (2, 4)))
    w_down = scatter_about(streams_of[10], (EXPERTS, HID, D), HID ** -0.5, 0.09375, ((0, 8), (1, 4)))
    return {"queries": queries, "keys": keys, "values": values, "stream": stream, "grad_out": grad_out, "norm_gain": norm_gain, "gate_probs": gate_probs, "routes": routes, "w_gate": w_gate, "w_up": w_up, "w_down": w_down}


EPSILON = 1e-06
HIGHEST = lax.Precision.HIGHEST

def expert_grads(xin, gin, weight_gate, weight_up, weight_down):
    gate_pre = jnp.dot(xin, weight_gate, preferred_element_type=jnp.float32)
    up_pre = jnp.dot(xin, weight_up, preferred_element_type=jnp.float32)
    sigmoid_g = jax.nn.sigmoid(gate_pre)
    silu_g = gate_pre * sigmoid_g
    acted = (silu_g * up_pre).astype(jnp.bfloat16)
    dact = jnp.dot(gin, weight_down.T, preferred_element_type=jnp.float32)
    down_grad = jnp.dot(acted.T, gin, preferred_element_type=jnp.float32)
    dgate = (dact * up_pre * sigmoid_g * (1.0 + gate_pre * (1.0 - sigmoid_g))).astype(jnp.bfloat16)
    dup = (dact * silu_g).astype(jnp.bfloat16)
    gate_grad = jnp.dot(xin.T, dgate, preferred_element_type=jnp.float32)
    up_grad = jnp.dot(xin.T, dup, preferred_element_type=jnp.float32)
    dxin = jnp.dot(dgate, weight_gate.T, preferred_element_type=jnp.float32) + jnp.dot(dup, weight_up.T, preferred_element_type=jnp.float32)
    return (dxin, gate_grad, up_grad, down_grad)

def attend_grads(query_rows, key_rows, value_rows, grad_rows, allowed):
    n_query = query_rows.shape[0]
    n_key = key_rows.shape[0]
    score_scale = 1.0 / math.sqrt(HEAD)
    q_three = query_rows.astype(jnp.float32).reshape(n_query, HEADS, HEAD)
    k_three = key_rows.astype(jnp.float32).reshape(n_key, HEADS, HEAD)
    v_three = value_rows.astype(jnp.float32).reshape(n_key, HEADS, HEAD)
    o_three = grad_rows.astype(jnp.float32).reshape(n_query, HEADS, HEAD)
    scores = jnp.einsum('qhd,khd->hqk', q_three, k_three, precision=HIGHEST) * score_scale
    scores = jnp.where(allowed[None], scores, -jnp.inf)
    row_max = lax.optimization_barrier(jnp.max(scores, -1, keepdims=True))
    exp_scores = jnp.exp(scores - row_max)
    probabilities = exp_scores / lax.optimization_barrier(jnp.sum(exp_scores, -1, keepdims=True))
    pround = probabilities.astype(jnp.bfloat16).astype(jnp.float32)
    attn = jnp.einsum('hqk,khd->qhd', pround, v_three, precision=HIGHEST)
    row_delta = lax.optimization_barrier(jnp.sum(o_three * attn, -1))
    dprob = jnp.einsum('qhd,khd->hqk', o_three, v_three, precision=HIGHEST)
    dscore = (probabilities * (dprob - row_delta.T[:, :, None])).astype(jnp.bfloat16).astype(jnp.float32)
    grad_q = jnp.einsum('hqk,khd->qhd', dscore, k_three, precision=HIGHEST) * score_scale
    grad_k = jnp.einsum('hqk,qhd->khd', dscore, q_three, precision=HIGHEST) * score_scale
    grad_v = jnp.einsum('hqk,qhd->khd', pround, o_three, precision=HIGHEST)
    return (grad_q.reshape(n_query, D), grad_k.reshape(n_key, D), grad_v.reshape(n_key, D))

def reference(queries, keys, values, stream, grad_out, norm_gain, gate_probs, routes, w_gate, w_up, w_down):
    devices = N_TM * N_EP
    stream_f = stream.astype(jnp.float32)
    inverse_rms = lax.rsqrt(lax.optimization_barrier(jnp.mean(stream_f * stream_f, -1, keepdims=True)) + EPSILON)
    scaled = stream_f * inverse_rms
    normed = (scaled * norm_gain).astype(jnp.bfloat16)
    egrad = (gate_probs[:, :, None] * grad_out.astype(jnp.float32)[:, None, :]).astype(jnp.bfloat16)
    flat_routes = routes.reshape(devices, FR_DEV * TOPK)
    onehot = (flat_routes[:, :, None] == jnp.arange(EXPERTS, dtype=jnp.int32)[None, None, :]).astype(jnp.int32)
    before = jnp.cumsum(onehot, 1) - onehot
    slot_index = lax.optimization_barrier(jnp.sum(before * onehot, 2)).astype(jnp.int32)
    device_rows = (jnp.arange(devices, dtype=jnp.int32) * CAP)[:, None]
    destination = (flat_routes * (devices * CAP) + device_rows + slot_index).reshape(-1).astype(jnp.int32)
    rows_total = EXPERTS * devices * CAP
    buffer_x = jnp.zeros((rows_total, D), jnp.bfloat16).at[destination].set(jnp.repeat(normed, TOPK, axis=0))
    buffer_g = jnp.zeros((rows_total, D), jnp.bfloat16).at[destination].set(egrad.reshape(-1, D))

    def one_expert(operands):
        return expert_grads(*operands)
    dx_rows, gate_grad, up_grad, down_grad = lax.map(one_expert, (buffer_x.reshape(EXPERTS, devices * CAP, D), buffer_g.reshape(EXPERTS, devices * CAP, D), w_gate, w_up, w_down))
    dnormed = lax.optimization_barrier(jnp.sum(dx_rows.reshape(rows_total, D)[destination].reshape(FRAMES, TOPK, D), 1))
    weighted = dnormed * norm_gain
    dstream = inverse_rms * (weighted - scaled * lax.optimization_barrier(jnp.mean(weighted * scaled, -1, keepdims=True)))
    stream_grad = (grad_out.astype(jnp.float32) + dstream).astype(jnp.bfloat16)
    padded_k = jnp.concatenate([jnp.zeros((LEFT, D), jnp.bfloat16), keys], 0)
    padded_v = jnp.concatenate([jnp.zeros((LEFT, D), jnp.bfloat16), values], 0)
    window = LEFT + SPAN

    def block_step(carry, block_id):
        acc_k, acc_v = carry
        start = (block_id * SPAN).astype(jnp.int32)
        query_rows = lax.dynamic_slice_in_dim(queries, start, SPAN, 0)
        grad_rows = lax.dynamic_slice_in_dim(stream_grad, start, SPAN, 0)
        key_rows = lax.dynamic_slice_in_dim(padded_k, start, window, 0)
        value_rows = lax.dynamic_slice_in_dim(padded_v, start, window, 0)
        key_pos = start - LEFT + jnp.arange(window, dtype=jnp.int32)
        allowed = jnp.broadcast_to((key_pos >= 0)[None, :], (SPAN, window))
        grad_q, grad_k, grad_v = attend_grads(query_rows, key_rows, value_rows, grad_rows, allowed)
        old_k = lax.dynamic_slice_in_dim(acc_k, start, window, 0)
        old_v = lax.dynamic_slice_in_dim(acc_v, start, window, 0)
        acc_k = lax.dynamic_update_slice_in_dim(acc_k, old_k + grad_k, start, 0)
        acc_v = lax.dynamic_update_slice_in_dim(acc_v, old_v + grad_v, start, 0)
        return ((acc_k, acc_v), grad_q.astype(jnp.bfloat16))
    start_carry = (jnp.zeros((LEFT + FRAMES, D), jnp.float32), jnp.zeros((LEFT + FRAMES, D), jnp.float32))
    (acc_k, acc_v), grad_blocks = lax.scan(block_step, start_carry, jnp.arange(FRAMES // SPAN, dtype=jnp.int32))
    queries_grad = grad_blocks.reshape(FRAMES, D)
    keys_grad = acc_k[LEFT:].astype(jnp.bfloat16)
    values_grad = acc_v[LEFT:].astype(jnp.bfloat16)
    return (queries_grad, keys_grad, values_grad, stream_grad, gate_grad, up_grad, down_grad)
```

```python
import functools
import math

import jax
import jax.numpy as jnp
from jax import lax
from jax.experimental import pallas as pl
from jax.experimental.pallas import tpu as pltpu
from jax.sharding import PartitionSpec as P

D = 1024
HEADS = 16
HEAD = 64
SPAN = 64
LEFT = 256


EPSILON = 1e-06


def shifted(block, axis, distance):
    devices = range(lax.axis_size(axis))
    route = [(i - distance, i) for i in devices if i - distance in devices]
    return lax.ppermute(block, axis, route)


MESH = pl.DeviceIdType.MESH
CHUNKS = 4
TILE = 256


def nt(a, b):
    return lax.dot_general(a, b, (((1,), (1,)), ((), ())), preferred_element_type=jnp.float32)


def tn(a, b):
    return lax.dot_general(a, b, (((0,), (0,)), ((), ())), preferred_element_type=jnp.float32)


def expert_kernel(
    n, cap,
    pick_ref, pick_t_ref, prob_ref, stream_ref, grad_ref, gain_ref, wg_hbm, wu_hbm, wd_hbm,
    sgrad_ref, gg_hbm, ug_hbm, dg_hbm,
    norm_s, send, xg, wg, wu, wd, acted, dgate, dup, part, from_core, from_x, back, grads,
    w_sem, out_sem, loc_sem, d_send, d_recv, a_send, a_recv, b_send, b_recv, c_send, c_recv,
):
    i = lax.axis_index("tm")
    j = lax.axis_index("ep")
    j1 = j + 1 - 2 * (j % 2)
    j2 = (j + 2) % 4
    j3 = (j1 + 2) % 4
    width = stream_ref.shape[1]
    hidden = wg.shape[1]
    per = n // CHUNKS
    rows = per * 4 * cap

    weights = [
        pltpu.make_async_copy(src, dst, w_sem.at[q])
        for q, (src, dst) in enumerate(((wg_hbm, wg), (wu_hbm, wu), (wd_hbm, wd)))
    ]
    for copy in weights:
        copy.start()

    barrier = pltpu.get_barrier_semaphore()
    for d in range(1, n):
        pl.semaphore_signal(barrier, inc=1, device_id=((i + d) % n, j), device_id_type=MESH)
    pl.semaphore_signal(barrier, inc=1, device_id=(i, j1), device_id_type=MESH)
    pl.semaphore_signal(barrier, inc=1, device_id=(i, j2), device_id_type=MESH)

    stream_f = stream_ref[...].astype(jnp.float32)
    inverse_rms = lax.rsqrt(jnp.mean(stream_f * stream_f, -1, keepdims=True) + EPSILON)
    norm_s[...] = (stream_f * inverse_rms * gain_ref[...]).astype(jnp.bfloat16)

    pl.semaphore_wait(barrier, n + 1)

    def remote(src, dst, ssem, rsem, to):
        return pltpu.make_async_remote_copy(
            src_ref=src, dst_ref=dst, send_sem=ssem, recv_sem=rsem, device_id=to, device_id_type=MESH
        )

    def to_expert(d):
        return remote(send.at[d], xg.at[d, j], d_send.at[d, 0], d_recv.at[d, 0], ((i + d) % n, j))

    own_copy = pltpu.make_async_copy(send.at[0], xg.at[0, j], loc_sem)
    for d in list(range(1, n)) + [0]:
        e = (i + d) % n
        pick = pick_ref[e]
        send[d, 0] = jnp.dot(pick, norm_s[...], preferred_element_type=jnp.float32).astype(jnp.bfloat16)
        grad_rows = jnp.dot(pick, grad_ref[...], preferred_element_type=jnp.float32)
        send[d, 1] = (grad_rows * prob_ref[e]).astype(jnp.bfloat16)
        if d:
            to_expert(d).start()
        else:
            own_copy.start()

    def own_to_core(d):
        return remote(xg.at[d, j], xg.at[d, j], d_send.at[d, 1], d_recv.at[d, 1], (i, j1))

    def own_to_x(d):
        return remote(xg.at[d, j], xg.at[d, j], d_send.at[d, 2], d_recv.at[d, 2], (i, j2))

    def x_to_core(d):
        return remote(xg.at[d, j2], xg.at[d, j2], d_send.at[d, 3], d_recv.at[d, 3], (i, j1))

    def span(c):
        return range(c * per, (c + 1) * per)

    def forward_own(c):
        for d in span(c):
            if d:
                to_expert(d).wait_recv()
            else:
                own_copy.wait()
            own_to_x(d).start()
            own_to_core(d).start()

    def forward_x(c):
        for d in span(c):
            own_to_x(d).wait_recv()
            x_to_core(d).start()

    def gather(c):
        for d in span(c):
            own_to_core(d).wait_recv()
            x_to_core(d).wait_recv()

    def compute(c):
        here = pl.ds(c * rows, rows)

        @pl.loop(0, hidden // TILE)
        def _(t):
            cols = pl.ds(pl.multiple_of(t * TILE, TILE), TILE)
            x = xg[c * per : (c + 1) * per, :, 0].reshape(rows, width)
            g = xg[c * per : (c + 1) * per, :, 1].reshape(rows, width)
            gate_pre = jnp.dot(x, wg[:, cols], preferred_element_type=jnp.float32)
            up_pre = jnp.dot(x, wu[:, cols], preferred_element_type=jnp.float32)
            dact = nt(g, wd[cols, :])
            sig = jax.nn.sigmoid(gate_pre)
            silu = gate_pre * sig
            acted[here, cols] = (silu * up_pre).astype(jnp.bfloat16)
            dgate[here, cols] = (dact * up_pre * sig * (1.0 + gate_pre * (1.0 - sig))).astype(jnp.bfloat16)
            dup[here, cols] = (dact * silu).astype(jnp.bfloat16)

        @pl.loop(0, width // TILE)
        def _(t):
            cols = pl.ds(pl.multiple_of(t * TILE, TILE), TILE)
            dx = nt(dgate[here, :], wg[cols, :]) + nt(dup[here, :], wu[cols, :])
            part[c * per : (c + 1) * per, :, :, cols] = dx.astype(jnp.bfloat16).reshape(per, 4, cap, TILE)

    def core_copies(d):
        return (
            remote(part.at[d, j1], from_core.at[d, 0], a_send.at[d, 0], a_recv.at[d, 0], (i, j1)),
            remote(part.at[d, j3], from_core.at[d, 1], a_send.at[d, 1], a_recv.at[d, 1], (i, j1)),
        )

    def x_copy(d):
        return remote(part.at[d, j2], from_x.at[d], b_send.at[d], b_recv.at[d], (i, j2))

    def home_copy(d):
        return remote(part.at[d, j], back.at[i], c_send.at[d], c_recv.at[d], ((i + n - d) % n, j))

    def stage_a(c):
        for d in span(c):
            for copy in core_copies(d):
                copy.start()

    def stage_b(c):
        for d in span(c):
            core_copies(d)[1].wait_recv()
            total = part[d, j2].astype(jnp.float32) + from_core[d, 1].astype(jnp.float32)
            part[d, j2] = total.astype(jnp.bfloat16)
            x_copy(d).start()

    def stage_c(c):
        for d in span(c):
            core_copies(d)[0].wait_recv()
            x_copy(d).wait_recv()
            total = part[d, j].astype(jnp.float32) + from_core[d, 0].astype(jnp.float32)
            total = (total + from_x[d].astype(jnp.float32)).astype(jnp.bfloat16)
            if d:
                part[d, j] = total
                home_copy(d).start()
            else:
                back[i] = total

    forward_own(0)
    for copy in weights:
        copy.wait()
    forward_own(1)
    for c in range(CHUNKS):
        forward_x(c)
        gather(c)
        compute(c)
        stage_a(c)
        if c + 2 < CHUNKS:
            forward_own(c + 2)
        if c >= 1:
            stage_b(c - 1)
        if c >= 2:
            stage_c(c - 2)
    stage_b(CHUNKS - 1)

    total_rows = n * 4 * cap
    writes = [
        pltpu.make_async_copy(grads.at[q], dst, out_sem.at[q]) for q, dst in enumerate((dg_hbm, gg_hbm, ug_hbm))
    ]

    @pl.loop(0, hidden // TILE)
    def _(t):
        cols = pl.ds(pl.multiple_of(t * TILE, TILE), TILE)
        lhs = acted[:, cols]
        for q in range(0, width, 512):
            rhs = xg[:, :, 1, :, q : q + 512].reshape(total_rows, 512)
            grads[0, cols, q : q + 512] = tn(lhs, rhs)

    writes[0].start()
    stage_c(CHUNKS - 2)
    stage_c(CHUNKS - 1)

    @pl.loop(0, width // TILE)
    def _(t):
        cols = pl.ds(pl.multiple_of(t * TILE, TILE), TILE)
        lhs = xg[:, :, 0, :, cols].reshape(total_rows, TILE)
        for q in range(0, hidden, 512):
            grads[1, cols, q : q + 512] = tn(lhs, dgate[:, q : q + 512])
            grads[2, cols, q : q + 512] = tn(lhs, dup[:, q : q + 512])

    writes[1].start()
    writes[2].start()

    for d in range(1, n):
        home_copy(d).wait_recv()
    dnormed = jnp.dot(pick_t_ref[...], back[...].reshape(n * cap, width), preferred_element_type=jnp.float32)
    stream_f = stream_ref[...].astype(jnp.float32)
    inverse_rms = lax.rsqrt(jnp.mean(stream_f * stream_f, -1, keepdims=True) + EPSILON)
    scaled = stream_f * inverse_rms
    weighted = dnormed * gain_ref[...]
    dstream = inverse_rms * (weighted - scaled * jnp.mean(weighted * scaled, -1, keepdims=True))
    sgrad_ref[...] = (grad_ref[...].astype(jnp.float32) + dstream).astype(jnp.bfloat16)

    for d in range(n):
        if d:
            to_expert(d).wait_send()
            home_copy(d).wait_send()
        own_to_core(d).wait_send()
        own_to_x(d).wait_send()
        x_to_core(d).wait_send()
        for copy in core_copies(d):
            copy.wait_send()
        x_copy(d).wait_send()
    for copy in writes:
        copy.wait()


def expert_part(n, cap, pick, pick_t, prob, stream, grad_out, gain, w_gate, w_up, w_down):
    frames, width = stream.shape
    hidden = w_gate.shape[1]
    total = n * 4 * cap
    bf, f32 = jnp.bfloat16, jnp.float32
    vmem = pl.BlockSpec(memory_space=pltpu.VMEM)
    hbm = pl.BlockSpec(memory_space=pl.ANY)
    dma = pltpu.SemaphoreType.DMA
    return pl.pallas_call(
        functools.partial(expert_kernel, n, cap),
        out_shape=(
            jax.ShapeDtypeStruct((frames, width), bf),
            jax.ShapeDtypeStruct((width, hidden), f32),
            jax.ShapeDtypeStruct((width, hidden), f32),
            jax.ShapeDtypeStruct((hidden, width), f32),
        ),
        in_specs=[vmem] * 6 + [hbm] * 3,
        out_specs=(vmem, hbm, hbm, hbm),
        scratch_shapes=[
            pltpu.VMEM((frames, width), bf),
            pltpu.VMEM((n, 2, cap, width), bf),
            pltpu.VMEM((n, 4, 2, cap, width), bf),
            pltpu.VMEM((width, hidden), bf),
            pltpu.VMEM((width, hidden), bf),
            pltpu.VMEM((hidden, width), bf),
            pltpu.VMEM((total, hidden), bf),
            pltpu.VMEM((total, hidden), bf),
            pltpu.VMEM((total, hidden), bf),
            pltpu.VMEM((n, 4, cap, width), bf),
            pltpu.VMEM((n, 2, cap, width), bf),
            pltpu.VMEM((n, cap, width), bf),
            pltpu.VMEM((n, cap, width), bf),
            pltpu.VMEM((3, width, hidden), f32),
            dma((3,)),
            dma((3,)),
            dma,
            dma((n, 4)),
            dma((n, 4)),
            dma((n, 2)),
            dma((n, 2)),
            dma((n,)),
            dma((n,)),
            dma((n,)),
            dma((n,)),
        ],
        compiler_params=pltpu.CompilerParams(
            collective_id=0, has_side_effects=True, vmem_limit_bytes=60 * 1024 * 1024
        ),
        cost_estimate=pl.CostEstimate(
            flops=16 * total * width * hidden, bytes_accessed=20 * width * hidden, transcendentals=0
        ),
    )(pick, pick_t, prob, stream, grad_out, gain, w_gate, w_up, w_down)


def attend_grads(query_rows, key_rows, value_rows, grad_rows, allowed):
    n_query = query_rows.shape[0]
    n_key = key_rows.shape[0]
    score_scale = 1.0 / math.sqrt(HEAD)
    q_three = query_rows.reshape(n_query, HEADS, HEAD)
    k_three = key_rows.reshape(n_key, HEADS, HEAD)
    v_three = value_rows.reshape(n_key, HEADS, HEAD)
    o_three = grad_rows.reshape(n_query, HEADS, HEAD)
    scores = (
        jnp.einsum("qhd,khd->hqk", q_three, k_three, preferred_element_type=jnp.float32)
        * score_scale
    )
    scores = jnp.where(allowed[None], scores, -jnp.inf)
    row_max = jnp.max(scores, -1, keepdims=True)
    exp_scores = jnp.exp(scores - row_max)
    probabilities = exp_scores / jnp.sum(exp_scores, -1, keepdims=True)
    pround = probabilities.astype(jnp.bfloat16)
    attn = jnp.einsum("hqk,khd->qhd", pround, v_three, preferred_element_type=jnp.float32)
    row_delta = jnp.sum(o_three.astype(jnp.float32) * attn, -1)
    dprob = jnp.einsum("qhd,khd->hqk", o_three, v_three, preferred_element_type=jnp.float32)
    dscore = (probabilities * (dprob - row_delta.T[:, :, None])).astype(jnp.bfloat16)
    grad_q = (
        jnp.einsum("hqk,khd->qhd", dscore, k_three, preferred_element_type=jnp.float32)
        * score_scale
    )
    grad_k = (
        jnp.einsum("hqk,qhd->khd", dscore, q_three, preferred_element_type=jnp.float32)
        * score_scale
    )
    grad_v = jnp.einsum("hqk,qhd->khd", pround, o_three, preferred_element_type=jnp.float32)
    return (grad_q.reshape(n_query, D), grad_k.reshape(n_key, D), grad_v.reshape(n_key, D))


def body(
    queries, keys, values, stream, grad_out, norm_gain, gate_probs, routes, w_gate, w_up, w_down
):
    frames = queries.shape[0]
    model_width = queries.shape[1]
    top_count = routes.shape[1]
    experts = lax.axis_size("tm")
    ep_count = lax.axis_size("ep")
    capacity = 3 * frames * top_count // (2 * experts)
    cap = -(-capacity // 16) * 16
    names = jnp.arange(experts, dtype=jnp.int32)[None, :]
    chosen = [(routes[:, k : k + 1] == names).astype(jnp.float32) for k in range(top_count)]
    order = jnp.arange(frames, dtype=jnp.int32)
    earlier = (order[None, :] < order[:, None]).astype(jnp.bfloat16)
    before = jnp.dot(earlier, sum(chosen).astype(jnp.bfloat16), preferred_element_type=jnp.float32)
    row_ids = jnp.arange(experts * cap, dtype=jnp.int32)[:, None]
    hits = []
    for k in range(top_count):
        slot = jnp.sum(before * chosen[k], 1).astype(jnp.int32)
        hits.append((routes[:, k] * cap + slot)[None, :] == row_ids)
    pick = functools.reduce(jnp.logical_or, hits).astype(jnp.bfloat16)
    prob = sum(
        jnp.sum(jnp.where(hits[k], gate_probs[:, k][None, :], 0.0), 1, keepdims=True)
        for k in range(top_count)
    )
    stream_grad, gate_grad, up_grad, down_grad = expert_part(
        experts,
        cap,
        pick.reshape(experts, cap, frames),
        pick.T,
        prob.reshape(experts, cap, 1),
        stream,
        grad_out,
        norm_gain[None, :],
        w_gate[0],
        w_up[0],
        w_down[0],
    )
    reach = -(-LEFT // frames)
    arrived = [
        shifted((keys, values), ("tm", "ep"), reach - offset_index) for offset_index in range(reach)
    ]
    rim_keys = jnp.concatenate([piece[0] for piece in arrived], 0)
    rim_values = jnp.concatenate([piece[1] for piece in arrived], 0)
    key_rows = jnp.concatenate([rim_keys, keys], 0)
    value_rows = jnp.concatenate([rim_values, values], 0)
    position = lax.axis_index("tm") * ep_count + lax.axis_index("ep")
    base_frame = position * frames
    query_pos = base_frame + jnp.arange(frames, dtype=jnp.int32)
    key_pos = base_frame - LEFT + jnp.arange(LEFT + frames, dtype=jnp.int32)
    query_span = query_pos // SPAN
    allowed = jnp.logical_and(
        key_pos[None, :] >= 0, key_pos[None, :] >= (query_span * SPAN - LEFT)[:, None]
    )
    allowed = jnp.logical_and(allowed, key_pos[None, :] < ((query_span + 1) * SPAN)[:, None])
    grad_q, grad_k, grad_v = attend_grads(queries, key_rows, value_rows, stream_grad, allowed)
    spare = reach * frames - LEFT
    padded_k = jnp.concatenate([jnp.zeros((spare, model_width), jnp.float32), grad_k[:LEFT]], 0)
    padded_v = jnp.concatenate([jnp.zeros((spare, model_width), jnp.float32), grad_v[:LEFT]], 0)
    sent_back = [
        (
            shifted(
                padded_k[offset_index * frames : (offset_index + 1) * frames].astype(jnp.bfloat16),
                ("tm", "ep"),
                offset_index - reach,
            ).astype(jnp.float32),
            shifted(
                padded_v[offset_index * frames : (offset_index + 1) * frames].astype(jnp.bfloat16),
                ("tm", "ep"),
                offset_index - reach,
            ).astype(jnp.float32),
        )
        for offset_index in range(reach)
    ]
    keys_total = grad_k[LEFT:]
    values_total = grad_v[LEFT:]
    for piece in sent_back:
        keys_total = keys_total + piece[0]
        values_total = values_total + piece[1]
    return (
        grad_q.astype(jnp.bfloat16),
        keys_total.astype(jnp.bfloat16),
        values_total.astype(jnp.bfloat16),
        stream_grad,
        gate_grad[None],
        up_grad[None],
        down_grad[None],
    )


def solution(mesh):
    return jax.shard_map(
        body,
        mesh=mesh,
        in_specs=(
            P(("tm", "ep"), None),
            P(("tm", "ep"), None),
            P(("tm", "ep"), None),
            P(("tm", "ep"), None),
            P(("tm", "ep"), None),
            P(),
            P(("tm", "ep"), None),
            P(("tm", "ep"), None),
            P("tm", None, "ep"),
            P("tm", None, "ep"),
            P("tm", "ep", None),
        ),
        out_specs=(
            P(("tm", "ep"), None),
            P(("tm", "ep"), None),
            P(("tm", "ep"), None),
            P(("tm", "ep"), None),
            P("tm", None, "ep"),
            P("tm", None, "ep"),
            P("tm", "ep", None),
        ),
        check_vma=False,
    )
```

```python
import functools
import math

import jax
import jax.numpy as jnp
from jax import lax
from jax.experimental import pallas as pl
from jax.experimental.pallas import tpu as pltpu
from jax.sharding import PartitionSpec as P

D = 1024
HEADS = 16
HEAD = 64
SPAN = 64
LEFT = 256


EPSILON = 1e-06


MESH = pl.DeviceIdType.MESH
CHUNKS = 4
TILE = 256


def nt(a, b):
    return lax.dot_general(a, b, (((1,), (1,)), ((), ())), preferred_element_type=jnp.float32)


def tn(a, b):
    return lax.dot_general(a, b, (((0,), (0,)), ((), ())), preferred_element_type=jnp.float32)


def expert_kernel(
    n, cap,
    route_ref, q_ref, k_ref, v_ref, stream_ref, grad_ref, gain_ref, wg_hbm, wu_hbm, wd_hbm,
    gq_ref, gk_ref, gv_ref, sgrad_ref, gg_hbm, ug_hbm, dg_hbm,
    pick, norm_s, send, kv, halo_out, halo_in, own, xg, wg, wu, wd, acted, dgate, dup, part, from_core, from_x, back, grads,
    w_sem, out_sem, loc_sem, d_send, d_recv, a_send, a_recv, b_send, b_recv, c_send, c_recv,
    kv_send, kv_recv, h_send, h_recv,
):
    i = lax.axis_index("tm")
    j = lax.axis_index("ep")
    j1 = j + 1 - 2 * (j % 2)
    j2 = (j + 2) % 4
    j3 = (j1 + 2) % 4
    width = stream_ref.shape[1]
    hidden = wg.shape[1]
    frames = stream_ref.shape[0]
    per = n // CHUNKS
    rows = per * 4 * cap

    weights = [
        pltpu.make_async_copy(src, dst, w_sem.at[q])
        for q, (src, dst) in enumerate(((wg_hbm, wg), (wu_hbm, wu), (wd_hbm, wd)))
    ]
    for copy in weights:
        copy.start()

    place = i * 4 + j
    places = n * 4

    def at(q):
        return (q // 4, q % 4)

    def nearby(act):
        for away in (1, 2):
            pl.when(place + away < places)(functools.partial(act, place + away))
            pl.when(place >= away)(functools.partial(act, place - away))

    barrier = pltpu.get_barrier_semaphore()
    nearby(lambda q: pl.semaphore_signal(barrier, inc=1, device_id=at(q), device_id_type=MESH))
    for d in range(1, n):
        pl.semaphore_signal(barrier, inc=1, device_id=((i + d) % n, j), device_id_type=MESH)
    pl.semaphore_signal(barrier, inc=1, device_id=(i, j1), device_id_type=MESH)
    pl.semaphore_signal(barrier, inc=1, device_id=(i, j2), device_id_type=MESH)

    stream_f = stream_ref[...].astype(jnp.float32)
    inverse_rms = lax.rsqrt(jnp.mean(stream_f * stream_f, -1, keepdims=True) + EPSILON)
    norm_s[...] = (stream_f * inverse_rms * gain_ref[...]).astype(jnp.bfloat16)

    kv[0, 2] = k_ref[...]
    kv[1, 2] = v_ref[...]

    names = lax.broadcasted_iota(jnp.int32, (n, frames), 0).astype(jnp.float32)
    chosen = [(names == route_ref[h : h + 1, :]).astype(jnp.float32) for h in range(2)]
    first = lax.broadcasted_iota(jnp.int32, (frames, frames), 0)
    second = lax.broadcasted_iota(jnp.int32, (frames, frames), 1)
    earlier = (first < second).astype(jnp.float32).astype(jnp.bfloat16)
    before = jnp.dot(
        (chosen[0] + chosen[1]).astype(jnp.bfloat16), earlier, preferred_element_type=jnp.float32
    )
    row_of = [
        route_ref[h : h + 1, :] * float(cap) + jnp.sum(before * chosen[h], 0, keepdims=True) for h in range(2)
    ]

    ahead = jnp.minimum(places - 1 - place, 2)
    pl.semaphore_wait(barrier, n + 1 + ahead + jnp.minimum(place, 2))

    def remote(src, dst, ssem, rsem, to):
        return pltpu.make_async_remote_copy(
            src_ref=src, dst_ref=dst, send_sem=ssem, recv_sem=rsem, device_id=to, device_id_type=MESH
        )

    def to_expert(d):
        return remote(send.at[d], xg.at[d, j], d_send.at[d, 0], d_recv.at[d, 0], ((i + d) % n, j))

    own_copy = pltpu.make_async_copy(send.at[0], xg.at[0, j], loc_sem)
    for d in list(range(1, n)) + [0]:
        e = (i + d) % n
        row_ids = (lax.broadcasted_iota(jnp.int32, (cap, frames), 0) + e * cap).astype(jnp.float32)
        hits = [(row_ids == row_of[h]).astype(jnp.float32) for h in range(2)]
        chance = sum(jnp.sum(hits[h] * route_ref[2 + h : 3 + h, :], 1, keepdims=True) for h in range(2))
        choice = (hits[0] + hits[1]).astype(jnp.bfloat16)
        pick[e] = choice
        send[d, 0] = jnp.dot(choice, norm_s[...], preferred_element_type=jnp.float32).astype(jnp.bfloat16)
        grad_rows = jnp.dot(choice, grad_ref[...], preferred_element_type=jnp.float32)
        send[d, 1] = (grad_rows * chance).astype(jnp.bfloat16)
        if d:
            to_expert(d).start()
        else:
            own_copy.start()

    even = j % 2 == 0

    def kv_all(away):
        return [
            remote(
                kv.at[q, 2], kv.at[q, 2 - away], kv_send.at[q, away], kv_recv.at[q, 2 - away], at(place + away)
            )
            for q in range(2)
        ]

    def kv_forwards():
        return [
            remote(kv.at[q, 1], kv.at[q, 0], kv_send.at[q, 0], kv_recv.at[q, 0], at(place + 1))
            for q in range(2)
        ]

    def each(copies, what):
        for copy in copies:
            getattr(copy, what)()

    has_next = place + 1 < places
    has_second = place + 2 < places

    @pl.when(has_next)
    def _():
        each(kv_all(1), "start")

    @pl.when(jnp.logical_and(even, has_second))
    def _():
        each(kv_all(2), "start")

    def kv_forward():
        @pl.when(place >= 1)
        def _():
            each(kv_all(1), "wait_recv")

        @pl.when(place < 1)
        def _():
            kv[:, 1] = jnp.zeros_like(kv[:, 1])

        @pl.when(jnp.logical_and(even, place >= 1))
        def _():
            each(kv_forwards(), "start")

    def kv_finish():
        @pl.when(place >= 2)
        def _():
            each(kv_all(2), "wait_recv")

        @pl.when(place < 2)
        def _():
            kv[:, 0] = jnp.zeros_like(kv[:, 0])

    scale = 1.0 / math.sqrt(HEAD)
    lane = lax.broadcasted_iota(jnp.int32, (1, 2 * HEAD), 1)
    low = (lane < HEAD).astype(jnp.float32).astype(jnp.bfloat16)
    high = (lane >= HEAD).astype(jnp.float32).astype(jnp.bfloat16)
    reach = LEFT + frames

    def paired(block):
        return jnp.concatenate([block * low, block * high], 0)

    def pair_columns(t):
        return pl.ds(pl.multiple_of(t * 2 * HEAD, 2 * HEAD), 2 * HEAD)

    def attend(begin, stop):
        row = lax.broadcasted_iota(jnp.int32, (2 * frames, reach), 0)
        col = lax.broadcasted_iota(jnp.int32, (2 * frames, reach), 1)
        start = (row % frames) // SPAN * SPAN
        seen = jnp.logical_and(col >= start, col < start + SPAN + LEFT)
        seen = jnp.logical_and(seen, col >= LEFT - place * frames)

        @pl.loop(begin, stop)
        def _(t):
            cols = pair_columns(t)
            keys = kv[0, :, :, cols].reshape(reach, 2 * HEAD)
            scores = nt(paired(q_ref[:, cols]), keys) * scale
            scores = jnp.where(seen, scores, -jnp.inf)
            exps = jnp.exp(scores - jnp.max(scores, -1, keepdims=True))
            probs = exps / jnp.sum(exps, -1, keepdims=True)
            here = pl.ds(pl.multiple_of(t * frames, frames), frames)
            grads[1, here, 0:reach] = probs[:frames]
            grads[1, here, reach : 2 * reach] = probs[frames:]

    def attend_back():
        @pl.loop(0, width // (2 * HEAD))
        def _(t):
            cols = pair_columns(t)
            here = pl.ds(pl.multiple_of(t * frames, frames), frames)
            keys = kv[0, :, :, cols].reshape(reach, 2 * HEAD)
            vals = kv[1, :, :, cols].reshape(reach, 2 * HEAD)
            probs = jnp.concatenate([grads[1, here, 0:reach], grads[1, here, reach : 2 * reach]], 0)
            pround = probs.astype(jnp.bfloat16)
            outs = paired(sgrad_ref[:, cols])
            dprob = nt(outs, vals)
            row_delta = jnp.sum(pround.astype(jnp.float32) * dprob, -1, keepdims=True)
            dscore = (probs * (dprob - row_delta)).astype(jnp.bfloat16)
            gq = jnp.dot(dscore, keys, preferred_element_type=jnp.float32) * scale
            gq_ref[:, cols] = jnp.where(lane < HEAD, gq[:frames], gq[frames:]).astype(jnp.bfloat16)
            for q, total in ((0, tn(dscore, paired(q_ref[:, cols])) * scale), (1, tn(pround, outs))):
                for piece in range(2):
                    part_rows = total[piece * frames : (piece + 1) * frames]
                    halo_out[piece, q, :, cols] = part_rows.astype(jnp.bfloat16)
                own[q, :, cols] = total[LEFT:]

    def halo_copy(away):
        return remote(
            halo_out.at[2 - away], halo_in.at[2 - away], h_send.at[away - 1], h_recv.at[away - 1], at(place - away)
        )

    def own_to_core(d):
        return remote(xg.at[d, j], xg.at[d, j], d_send.at[d, 1], d_recv.at[d, 1], (i, j1))

    def own_to_x(d):
        return remote(xg.at[d, j], xg.at[d, j], d_send.at[d, 2], d_recv.at[d, 2], (i, j2))

    def x_to_core(d):
        return remote(xg.at[d, j2], xg.at[d, j2], d_send.at[d, 3], d_recv.at[d, 3], (i, j1))

    def span(c):
        return range(c * per, (c + 1) * per)

    def forward_own(c):
        for d in span(c):
            if d:
                to_expert(d).wait_recv()
            else:
                own_copy.wait()
            own_to_x(d).start()
            own_to_core(d).start()

    def forward_x(c):
        for d in span(c):
            own_to_x(d).wait_recv()
            x_to_core(d).start()

    def gather(c):
        for d in span(c):
            own_to_core(d).wait_recv()
            x_to_core(d).wait_recv()

    def compute(c):
        here = pl.ds(c * rows, rows)

        @pl.loop(0, hidden // TILE)
        def _(t):
            cols = pl.ds(pl.multiple_of(t * TILE, TILE), TILE)
            x = xg[c * per : (c + 1) * per, :, 0].reshape(rows, width)
            g = xg[c * per : (c + 1) * per, :, 1].reshape(rows, width)
            gate_pre = jnp.dot(x, wg[:, cols], preferred_element_type=jnp.float32)
            up_pre = jnp.dot(x, wu[:, cols], preferred_element_type=jnp.float32)
            dact = nt(g, wd[cols, :])
            sig = jax.nn.sigmoid(gate_pre)
            silu = gate_pre * sig
            acted[here, cols] = (silu * up_pre).astype(jnp.bfloat16)
            dgate[here, cols] = (dact * up_pre * sig * (1.0 + gate_pre * (1.0 - sig))).astype(jnp.bfloat16)
            dup[here, cols] = (dact * silu).astype(jnp.bfloat16)

        @pl.loop(0, width // TILE)
        def _(t):
            cols = pl.ds(pl.multiple_of(t * TILE, TILE), TILE)
            dx = nt(dgate[here, :], wg[cols, :]) + nt(dup[here, :], wu[cols, :])
            part[c * per : (c + 1) * per, :, :, cols] = dx.astype(jnp.bfloat16).reshape(per, 4, cap, TILE)

    def core_copies(d):
        return (
            remote(part.at[d, j1], from_core.at[d, 0], a_send.at[d, 0], a_recv.at[d, 0], (i, j1)),
            remote(part.at[d, j3], from_core.at[d, 1], a_send.at[d, 1], a_recv.at[d, 1], (i, j1)),
        )

    def x_copy(d):
        return remote(part.at[d, j2], from_x.at[d], b_send.at[d], b_recv.at[d], (i, j2))

    def home_copy(d):
        return remote(part.at[d, j], back.at[i], c_send.at[d], c_recv.at[d], ((i + n - d) % n, j))

    def stage_a(c):
        for d in span(c):
            for copy in core_copies(d):
                copy.start()

    def stage_b(c):
        for d in span(c):
            core_copies(d)[1].wait_recv()
            total = part[d, j2].astype(jnp.float32) + from_core[d, 1].astype(jnp.float32)
            part[d, j2] = total.astype(jnp.bfloat16)
            x_copy(d).start()

    def stage_c(c):
        for d in span(c):
            core_copies(d)[0].wait_recv()
            x_copy(d).wait_recv()
            total = part[d, j].astype(jnp.float32) + from_core[d, 0].astype(jnp.float32)
            total = (total + from_x[d].astype(jnp.float32)).astype(jnp.bfloat16)
            if d:
                part[d, j] = total
                home_copy(d).start()
            else:
                back[i] = total

    forward_own(0)
    for copy in weights:
        copy.wait()
    forward_own(1)
    for c in range(CHUNKS):
        forward_x(c)
        gather(c)
        compute(c)
        stage_a(c)
        if c + 2 < CHUNKS:
            forward_own(c + 2)
        if c >= 1:
            stage_b(c - 1)
        if c >= 2:
            stage_c(c - 2)
        if c == 1:
            kv_forward()
    kv_finish()
    pairs = width // (2 * HEAD)
    attend(0, pairs // 2)
    stage_b(CHUNKS - 1)
    stage_c(CHUNKS - 2)
    attend(pairs // 2, pairs)
    stage_c(CHUNKS - 1)

    total_rows = n * 4 * cap
    writes = [
        pltpu.make_async_copy(grads.at[q % 2], dst, out_sem.at[q])
        for q, dst in enumerate((dg_hbm, gg_hbm, ug_hbm))
    ]

    @pl.loop(0, hidden // TILE)
    def _(t):
        cols = pl.ds(pl.multiple_of(t * TILE, TILE), TILE)
        lhs = acted[:, cols]
        for q in range(0, width, 512):
            rhs = xg[:, :, 1, :, q : q + 512].reshape(total_rows, 512)
            grads[0, cols, q : q + 512] = tn(lhs, rhs)

    writes[0].start()
    for d in range(1, n):
        home_copy(d).wait_recv()
    dnormed = tn(pick[...].reshape(n * cap, frames), back[...].reshape(n * cap, width))
    stream_f = stream_ref[...].astype(jnp.float32)
    inverse_rms = lax.rsqrt(jnp.mean(stream_f * stream_f, -1, keepdims=True) + EPSILON)
    scaled = stream_f * inverse_rms
    weighted = dnormed * gain_ref[...]
    dstream = inverse_rms * (weighted - scaled * jnp.mean(weighted * scaled, -1, keepdims=True))
    sgrad_ref[...] = (grad_ref[...].astype(jnp.float32) + dstream).astype(jnp.bfloat16)

    attend_back()
    for away in (1, 2):
        @pl.when(place >= away)
        def _():
            halo_copy(away).start()

    writes[0].wait()

    @pl.loop(0, width // TILE)
    def _(t):
        cols = pl.ds(pl.multiple_of(t * TILE, TILE), TILE)
        lhs = xg[:, :, 0, :, cols].reshape(total_rows, TILE)
        for q in range(0, hidden, 512):
            grads[1, cols, q : q + 512] = tn(lhs, dgate[:, q : q + 512])
            grads[0, cols, q : q + 512] = tn(lhs, dup[:, q : q + 512])

    writes[1].start()
    writes[2].start()

    for away in (1, 2):
        @pl.when(place + away < places)
        def _():
            halo_copy(away).wait_recv()

        @pl.when(place + away >= places)
        def _():
            halo_in[2 - away] = jnp.zeros_like(halo_in[2 - away])

    for q, out_ref in ((0, gk_ref), (1, gv_ref)):
        total = own[q] + halo_in[0, q].astype(jnp.float32) + halo_in[1, q].astype(jnp.float32)
        out_ref[...] = total.astype(jnp.bfloat16)

    for away in (1, 2):
        @pl.when(place >= away)
        def _():
            halo_copy(away).wait_send()

    @pl.when(has_next)
    def _():
        each(kv_all(1), "wait_send")

    @pl.when(jnp.logical_and(even, has_second))
    def _():
        each(kv_all(2), "wait_send")

    @pl.when(jnp.logical_and(even, place >= 1))
    def _():
        each(kv_forwards(), "wait_send")

    for d in range(n):
        if d:
            to_expert(d).wait_send()
            home_copy(d).wait_send()
        own_to_core(d).wait_send()
        own_to_x(d).wait_send()
        x_to_core(d).wait_send()
        for copy in core_copies(d):
            copy.wait_send()
        x_copy(d).wait_send()
    for copy in writes[1:]:
        copy.wait()


def expert_part(n, cap, route, queries, keys, values, stream, grad_out, gain, w_gate, w_up, w_down):
    frames, width = stream.shape
    hidden = w_gate.shape[1]
    total = n * 4 * cap
    bf, f32 = jnp.bfloat16, jnp.float32
    vmem = pl.BlockSpec(memory_space=pltpu.VMEM)
    hbm = pl.BlockSpec(memory_space=pl.ANY)
    dma = pltpu.SemaphoreType.DMA
    return pl.pallas_call(
        functools.partial(expert_kernel, n, cap),
        out_shape=(
            jax.ShapeDtypeStruct((frames, width), bf),
            jax.ShapeDtypeStruct((frames, width), bf),
            jax.ShapeDtypeStruct((frames, width), bf),
            jax.ShapeDtypeStruct((frames, width), bf),
            jax.ShapeDtypeStruct((width, hidden), f32),
            jax.ShapeDtypeStruct((width, hidden), f32),
            jax.ShapeDtypeStruct((hidden, width), f32),
        ),
        in_specs=[vmem] * 7 + [hbm] * 3,
        out_specs=(vmem, vmem, vmem, vmem, hbm, hbm, hbm),
        scratch_shapes=[
            pltpu.VMEM((n, cap, frames), bf),
            pltpu.VMEM((frames, width), bf),
            pltpu.VMEM((n, 2, cap, width), bf),
            pltpu.VMEM((2, 3, frames, width), bf),
            pltpu.VMEM((2, 2, frames, width), bf),
            pltpu.VMEM((2, 2, frames, width), bf),
            pltpu.VMEM((2, frames, width), f32),
            pltpu.VMEM((n, 4, 2, cap, width), bf),
            pltpu.VMEM((width, hidden), bf),
            pltpu.VMEM((width, hidden), bf),
            pltpu.VMEM((hidden, width), bf),
            pltpu.VMEM((total, hidden), bf),
            pltpu.VMEM((total, hidden), bf),
            pltpu.VMEM((total, hidden), bf),
            pltpu.VMEM((n, 4, cap, width), bf),
            pltpu.VMEM((n, 2, cap, width), bf),
            pltpu.VMEM((n, cap, width), bf),
            pltpu.VMEM((n, cap, width), bf),
            pltpu.VMEM((2, width, hidden), f32),
            dma((3,)),
            dma((3,)),
            dma,
            dma((n, 4)),
            dma((n, 4)),
            dma((n, 2)),
            dma((n, 2)),
            dma((n,)),
            dma((n,)),
            dma((n,)),
            dma((n,)),
            dma((2, 3)),
            dma((2, 2)),
            dma((2,)),
            dma((2,)),
        ],
        compiler_params=pltpu.CompilerParams(
            collective_id=0, has_side_effects=True, vmem_limit_bytes=60 * 1024 * 1024
        ),
        cost_estimate=pl.CostEstimate(
            flops=16 * total * width * hidden, bytes_accessed=20 * width * hidden, transcendentals=0
        ),
    )(route, queries, keys, values, stream, grad_out, gain, w_gate, w_up, w_down)


def body(
    queries, keys, values, stream, grad_out, norm_gain, gate_probs, routes, w_gate, w_up, w_down
):
    frames = queries.shape[0]
    experts = lax.axis_size("tm")
    capacity = 3 * frames * routes.shape[1] // (2 * experts)
    cap = -(-capacity // 16) * 16
    route = jnp.concatenate([routes.astype(jnp.float32).T, gate_probs.T], 0)
    grad_q, grad_k, grad_v, stream_grad, gate_grad, up_grad, down_grad = expert_part(
        experts, cap, route, queries, keys, values, stream, grad_out, norm_gain[None, :],
        w_gate[0], w_up[0], w_down[0],
    )
    return (
        grad_q, grad_k, grad_v, stream_grad, gate_grad[None], up_grad[None], down_grad[None]
    )


def solution(mesh):
    return jax.shard_map(
        body,
        mesh=mesh,
        in_specs=(
            P(("tm", "ep"), None),
            P(("tm", "ep"), None),
            P(("tm", "ep"), None),
            P(("tm", "ep"), None),
            P(("tm", "ep"), None),
            P(),
            P(("tm", "ep"), None),
            P(("tm", "ep"), None),
            P("tm", None, "ep"),
            P("tm", None, "ep"),
            P("tm", "ep", None),
        ),
        out_specs=(
            P(("tm", "ep"), None),
            P(("tm", "ep"), None),
            P(("tm", "ep"), None),
            P(("tm", "ep"), None),
            P("tm", None, "ep"),
            P("tm", None, "ep"),
            P("tm", "ep", None),
        ),
        check_vma=False,
    )
```

```python
import functools
import math

import jax
import jax.numpy as jnp
from jax import lax
from jax.experimental import pallas as pl
from jax.experimental.pallas import tpu as pltpu
from jax.sharding import PartitionSpec as P

D = 1024
HEADS = 16
HEAD = 64
SPAN = 64
LEFT = 256


EPSILON = 1e-06


MESH = pl.DeviceIdType.MESH
CHUNKS = 4
TILE = 256


def nt(a, b):
    return lax.dot_general(a, b, (((1,), (1,)), ((), ())), preferred_element_type=jnp.float32)


def tn(a, b):
    return lax.dot_general(a, b, (((0,), (0,)), ((), ())), preferred_element_type=jnp.float32)


def expert_kernel(
    n, cap,
    route_ref, q_ref, k_ref, v_ref, stream_ref, grad_ref, gain_ref, wg_hbm, wu_hbm, wd_hbm,
    gq_ref, gk_ref, gv_ref, sgrad_ref, gg_hbm, dg_hbm, x_hbm, dup_hbm,
    pick, norm_s, send, kv, halo_out, halo_in, own, kept, xg, wg, wu, wd, acted, dgate, dup, part, from_core, from_x, back, grads,
    w_sem, out_sem, loc_sem, d_send, d_recv, a_send, a_recv, b_send, b_recv, c_send, c_recv,
    kv_send, kv_recv, h_send, h_recv,
):
    i = lax.axis_index("tm")
    j = lax.axis_index("ep")
    j1 = j + 1 - 2 * (j % 2)
    j2 = (j + 2) % 4
    j3 = (j1 + 2) % 4
    width = stream_ref.shape[1]
    hidden = wg.shape[1]
    frames = stream_ref.shape[0]
    per = n // CHUNKS
    rows = per * 4 * cap

    weights = [
        pltpu.make_async_copy(src, dst, w_sem.at[q])
        for q, (src, dst) in enumerate(((wg_hbm, wg), (wu_hbm, wu), (wd_hbm, wd)))
    ]
    for copy in weights:
        copy.start()

    place = i * 4 + j
    places = n * 4

    def at(q):
        return (q // 4, q % 4)

    def nearby(act):
        for away in (1, 2):
            pl.when(place + away < places)(functools.partial(act, place + away))
            pl.when(place >= away)(functools.partial(act, place - away))

    barrier = pltpu.get_barrier_semaphore()
    nearby(lambda q: pl.semaphore_signal(barrier, inc=1, device_id=at(q), device_id_type=MESH))
    for d in range(1, n):
        pl.semaphore_signal(barrier, inc=1, device_id=((i + d) % n, j), device_id_type=MESH)
    pl.semaphore_signal(barrier, inc=1, device_id=(i, j1), device_id_type=MESH)
    pl.semaphore_signal(barrier, inc=1, device_id=(i, j2), device_id_type=MESH)

    stream_f = stream_ref[...].astype(jnp.float32)
    inverse_rms = lax.rsqrt(jnp.mean(stream_f * stream_f, -1, keepdims=True) + EPSILON)
    norm_s[...] = (stream_f * inverse_rms * gain_ref[...]).astype(jnp.bfloat16)

    kv[0, 2] = k_ref[...]
    kv[1, 2] = v_ref[...]

    names = lax.broadcasted_iota(jnp.int32, (n, frames), 0).astype(jnp.float32)
    chosen = [(names == route_ref[h : h + 1, :]).astype(jnp.float32) for h in range(2)]
    first = lax.broadcasted_iota(jnp.int32, (frames, frames), 0)
    second = lax.broadcasted_iota(jnp.int32, (frames, frames), 1)
    earlier = (first < second).astype(jnp.float32).astype(jnp.bfloat16)
    before = jnp.dot(
        (chosen[0] + chosen[1]).astype(jnp.bfloat16), earlier, preferred_element_type=jnp.float32
    )
    row_of = [
        route_ref[h : h + 1, :] * float(cap) + jnp.sum(before * chosen[h], 0, keepdims=True) for h in range(2)
    ]

    ahead = jnp.minimum(places - 1 - place, 2)
    pl.semaphore_wait(barrier, n + 1 + ahead + jnp.minimum(place, 2))

    def remote(src, dst, ssem, rsem, to):
        return pltpu.make_async_remote_copy(
            src_ref=src, dst_ref=dst, send_sem=ssem, recv_sem=rsem, device_id=to, device_id_type=MESH
        )

    def to_expert(d):
        return remote(send.at[d], xg.at[d, j], d_send.at[d, 0], d_recv.at[d, 0], ((i + d) % n, j))

    even = j % 2 == 0

    def kv_all(away):
        return [
            remote(
                kv.at[q, 2], kv.at[q, 2 - away], kv_send.at[q, away], kv_recv.at[q, 2 - away], at(place + away)
            )
            for q in range(2)
        ]

    def kv_forwards():
        return [
            remote(kv.at[q, 1], kv.at[q, 0], kv_send.at[q, 0], kv_recv.at[q, 0], at(place + 1))
            for q in range(2)
        ]

    def each(copies, what):
        for copy in copies:
            getattr(copy, what)()

    has_next = place + 1 < places
    has_second = place + 2 < places

    @pl.when(has_next)
    def _():
        each(kv_all(1), "start")

    @pl.when(jnp.logical_and(even, has_second))
    def _():
        each(kv_all(2), "start")

    own_copy = pltpu.make_async_copy(send.at[0], xg.at[0, j], loc_sem)
    for d in list(range(1, n)) + [0]:
        e = (i + d) % n
        row_ids = (lax.broadcasted_iota(jnp.int32, (cap, frames), 0) + e * cap).astype(jnp.float32)
        hits = [(row_ids == row_of[h]).astype(jnp.float32) for h in range(2)]
        chance = sum(jnp.sum(hits[h] * route_ref[2 + h : 3 + h, :], 1, keepdims=True) for h in range(2))
        choice = (hits[0] + hits[1]).astype(jnp.bfloat16)
        pick[e] = choice
        send[d, 0] = jnp.dot(choice, norm_s[...], preferred_element_type=jnp.float32).astype(jnp.bfloat16)
        grad_rows = jnp.dot(choice, grad_ref[...], preferred_element_type=jnp.float32)
        send[d, 1] = (grad_rows * chance).astype(jnp.bfloat16)
        if d:
            to_expert(d).start()
        else:
            own_copy.start()

    def kv_forward():
        @pl.when(place >= 1)
        def _():
            each(kv_all(1), "wait_recv")

        @pl.when(place < 1)
        def _():
            kv[:, 1] = jnp.zeros_like(kv[:, 1])

        @pl.when(jnp.logical_and(even, place >= 1))
        def _():
            each(kv_forwards(), "start")

    def kv_finish():
        @pl.when(place >= 2)
        def _():
            each(kv_all(2), "wait_recv")

        @pl.when(place < 2)
        def _():
            kv[:, 0] = jnp.zeros_like(kv[:, 0])

    scale = 1.0 / math.sqrt(HEAD)
    lane = lax.broadcasted_iota(jnp.int32, (1, 2 * HEAD), 1)
    low = (lane < HEAD).astype(jnp.float32).astype(jnp.bfloat16)
    high = (lane >= HEAD).astype(jnp.float32).astype(jnp.bfloat16)
    reach = LEFT + frames

    def paired(block):
        return jnp.concatenate([block * low, block * high], 0)

    def pair_columns(t):
        return pl.ds(pl.multiple_of(t * 2 * HEAD, 2 * HEAD), 2 * HEAD)

    def attend(begin, stop):
        row = lax.broadcasted_iota(jnp.int32, (2 * frames, reach), 0)
        col = lax.broadcasted_iota(jnp.int32, (2 * frames, reach), 1)
        start = (row % frames) // SPAN * SPAN
        seen = jnp.logical_and(col >= start, col < start + SPAN + LEFT)
        seen = jnp.logical_and(seen, col >= LEFT - place * frames)

        @pl.loop(begin, stop)
        def _(t):
            cols = pair_columns(t)
            keys = kv[0, :, :, cols].reshape(reach, 2 * HEAD)
            scores = nt(paired(q_ref[:, cols]), keys) * scale
            scores = jnp.where(seen, scores, -jnp.inf)
            exps = jnp.exp(scores - jnp.max(scores, -1, keepdims=True))
            probs = exps / jnp.sum(exps, -1, keepdims=True)
            kept[t] = probs

    def attend_back():
        @pl.loop(0, width // (2 * HEAD))
        def _(t):
            cols = pair_columns(t)
            keys = kv[0, :, :, cols].reshape(reach, 2 * HEAD)
            vals = kv[1, :, :, cols].reshape(reach, 2 * HEAD)
            probs = kept[t]
            pround = probs.astype(jnp.bfloat16)
            outs = paired(sgrad_ref[:, cols])
            dprob = nt(outs, vals)
            row_delta = jnp.sum(pround.astype(jnp.float32) * dprob, -1, keepdims=True)
            dscore = (probs * (dprob - row_delta)).astype(jnp.bfloat16)
            gq = jnp.dot(dscore, keys, preferred_element_type=jnp.float32) * scale
            gq_ref[:, cols] = jnp.where(lane < HEAD, gq[:frames], gq[frames:]).astype(jnp.bfloat16)
            for q, total in ((0, tn(dscore, paired(q_ref[:, cols])) * scale), (1, tn(pround, outs))):
                for piece in range(2):
                    part_rows = total[piece * frames : (piece + 1) * frames]
                    halo_out[piece, q, :, cols] = part_rows.astype(jnp.bfloat16)
                own[q, :, cols] = total[LEFT:]

    def halo_copy(away):
        return remote(
            halo_out.at[2 - away], halo_in.at[2 - away], h_send.at[away - 1], h_recv.at[away - 1], at(place - away)
        )

    def own_to_core(d):
        return remote(xg.at[d, j], xg.at[d, j], d_send.at[d, 1], d_recv.at[d, 1], (i, j1))

    def own_to_x(d):
        return remote(xg.at[d, j], xg.at[d, j], d_send.at[d, 2], d_recv.at[d, 2], (i, j2))

    def x_to_core(d):
        return remote(xg.at[d, j2], xg.at[d, j2], d_send.at[d, 3], d_recv.at[d, 3], (i, j1))

    def span(c):
        return range(c * per, (c + 1) * per)

    def forward_own(c):
        for d in span(c):
            if d:
                to_expert(d).wait_recv()
            else:
                own_copy.wait()
            own_to_x(d).start()
            own_to_core(d).start()

    def forward_x(c):
        for d in span(c):
            own_to_x(d).wait_recv()
            x_to_core(d).start()

    def gather(c):
        for d in span(c):
            own_to_core(d).wait_recv()
            x_to_core(d).wait_recv()

    def compute(c):
        here = pl.ds(c * rows, rows)

        @pl.loop(0, hidden // TILE)
        def _(t):
            cols = pl.ds(pl.multiple_of(t * TILE, TILE), TILE)
            x = xg[c * per : (c + 1) * per, :, 0].reshape(rows, width)
            g = xg[c * per : (c + 1) * per, :, 1].reshape(rows, width)
            gate_pre = jnp.dot(x, wg[:, cols], preferred_element_type=jnp.float32)
            up_pre = jnp.dot(x, wu[:, cols], preferred_element_type=jnp.float32)
            dact = nt(g, wd[cols, :])
            sig = jax.nn.sigmoid(gate_pre)
            silu = gate_pre * sig
            acted[here, cols] = (silu * up_pre).astype(jnp.bfloat16)
            dgate[here, cols] = (dact * up_pre * sig * (1.0 + gate_pre * (1.0 - sig))).astype(jnp.bfloat16)
            dup[here, cols] = (dact * silu).astype(jnp.bfloat16)

        @pl.loop(0, width // TILE)
        def _(t):
            cols = pl.ds(pl.multiple_of(t * TILE, TILE), TILE)
            dx = nt(dgate[here, :], wg[cols, :]) + nt(dup[here, :], wu[cols, :])
            part[c * per : (c + 1) * per, :, :, cols] = dx.astype(jnp.bfloat16).reshape(per, 4, cap, TILE)

    def core_copies(d):
        return (
            remote(part.at[d, j1], from_core.at[d, 0], a_send.at[d, 0], a_recv.at[d, 0], (i, j1)),
            remote(part.at[d, j3], from_core.at[d, 1], a_send.at[d, 1], a_recv.at[d, 1], (i, j1)),
        )

    def x_copy(d):
        return remote(part.at[d, j2], from_x.at[d], b_send.at[d], b_recv.at[d], (i, j2))

    def home_copy(d):
        return remote(part.at[d, j], back.at[i], c_send.at[d], c_recv.at[d], ((i + n - d) % n, j))

    def stage_a(c):
        for d in span(c):
            for copy in core_copies(d):
                copy.start()

    def stage_b(c):
        for d in span(c):
            core_copies(d)[1].wait_recv()
            total = part[d, j2].astype(jnp.float32) + from_core[d, 1].astype(jnp.float32)
            part[d, j2] = total.astype(jnp.bfloat16)
            x_copy(d).start()

    def stage_c(c):
        for d in span(c):
            core_copies(d)[0].wait_recv()
            x_copy(d).wait_recv()
            total = part[d, j].astype(jnp.float32) + from_core[d, 0].astype(jnp.float32)
            total = (total + from_x[d].astype(jnp.float32)).astype(jnp.bfloat16)
            if d:
                part[d, j] = total
                home_copy(d).start()
            else:
                back[i] = total

    pairs = width // (2 * HEAD)
    forward_own(0)
    forward_own(1)
    kv_forward()
    for c in range(CHUNKS):
        forward_x(c)
        if c == 0:
            kv_finish()
            attend(0, pairs // 2)
            each(weights, "wait")
        if c == 1:
            attend(pairs // 2, pairs)
        if c >= 1:
            stage_b(c - 1)
        if c >= 2:
            stage_c(c - 2)
        gather(c)
        compute(c)
        stage_a(c)
        if c + 2 < CHUNKS:
            forward_own(c + 2)

    total_rows = n * 4 * cap
    writes = [
        pltpu.make_async_copy(grads.at[0], dg_hbm, out_sem.at[0]),
        pltpu.make_async_copy(grads.at[1], gg_hbm, out_sem.at[1]),
        pltpu.make_async_copy(xg.at[:, :, 0], x_hbm, out_sem.at[2]),
        pltpu.make_async_copy(dup, dup_hbm, out_sem.at[3]),
    ]
    writes[2].start()
    writes[3].start()

    def down_grads(begin, stop):
        @pl.loop(begin, stop)
        def _(t):
            cols = pl.ds(pl.multiple_of(t * TILE, TILE), TILE)
            lhs = acted[:, cols]
            for q in range(0, width, 512):
                rhs = xg[:, :, 1, :, q : q + 512].reshape(total_rows, 512)
                grads[0, cols, q : q + 512] = tn(lhs, rhs)

    def gate_grads(begin, stop):
        @pl.loop(begin, stop)
        def _(t):
            cols = pl.ds(pl.multiple_of(t * TILE, TILE), TILE)
            lhs = xg[:, :, 0, :, cols].reshape(total_rows, TILE)
            for q in range(0, hidden, 512):
                grads[1, cols, q : q + 512] = tn(lhs, dgate[:, q : q + 512])

    down_tiles = hidden // TILE
    gate_tiles = width // TILE
    down_grads(0, down_tiles // 2)
    stage_b(CHUNKS - 1)
    stage_c(CHUNKS - 2)
    down_grads(down_tiles // 2, down_tiles)
    writes[0].start()
    stage_c(CHUNKS - 1)
    gate_grads(0, gate_tiles // 2)

    for d in range(1, n):
        home_copy(d).wait_recv()
    dnormed = tn(pick[...].reshape(n * cap, frames), back[...].reshape(n * cap, width))
    stream_f = stream_ref[...].astype(jnp.float32)
    inverse_rms = lax.rsqrt(jnp.mean(stream_f * stream_f, -1, keepdims=True) + EPSILON)
    scaled = stream_f * inverse_rms
    weighted = dnormed * gain_ref[...]
    dstream = inverse_rms * (weighted - scaled * jnp.mean(weighted * scaled, -1, keepdims=True))
    sgrad_ref[...] = (grad_ref[...].astype(jnp.float32) + dstream).astype(jnp.bfloat16)

    attend_back()
    for away in (1, 2):
        @pl.when(place >= away)
        def _():
            halo_copy(away).start()

    gate_grads(gate_tiles // 2, gate_tiles)
    writes[1].start()

    for away in (1, 2):
        @pl.when(place + away < places)
        def _():
            halo_copy(away).wait_recv()

        @pl.when(place + away >= places)
        def _():
            halo_in[2 - away] = jnp.zeros_like(halo_in[2 - away])

    for q, out_ref in ((0, gk_ref), (1, gv_ref)):
        total = own[q] + halo_in[0, q].astype(jnp.float32) + halo_in[1, q].astype(jnp.float32)
        out_ref[...] = total.astype(jnp.bfloat16)

    for away in (1, 2):
        @pl.when(place >= away)
        def _():
            halo_copy(away).wait_send()

    @pl.when(has_next)
    def _():
        each(kv_all(1), "wait_send")

    @pl.when(jnp.logical_and(even, has_second))
    def _():
        each(kv_all(2), "wait_send")

    @pl.when(jnp.logical_and(even, place >= 1))
    def _():
        each(kv_forwards(), "wait_send")

    for d in range(n):
        if d:
            to_expert(d).wait_send()
            home_copy(d).wait_send()
        own_to_core(d).wait_send()
        own_to_x(d).wait_send()
        x_to_core(d).wait_send()
        for copy in core_copies(d):
            copy.wait_send()
        x_copy(d).wait_send()
    each(writes, "wait")


def finish_kernel(x_ref, dup_ref, *refs):
    half = len(refs) // 2
    refs[half][...] = tn(x_ref[...], dup_ref[...])
    for src, dst in zip(refs[:half], refs[half + 1 :]):
        dst[...] = src[...]


def finish(x_rows, dup_rows, passed):
    total, width = x_rows.shape
    hidden = dup_rows.shape[1]
    steps = width // TILE
    blocks = [pl.BlockSpec((a.shape[0] // steps, a.shape[1]), lambda t: (t, 0)) for a in passed]
    up_block = pl.BlockSpec((TILE, hidden), lambda t: (t, 0))
    return pl.pallas_call(
        finish_kernel,
        grid=(steps,),
        out_shape=[jax.ShapeDtypeStruct((width, hidden), jnp.float32)]
        + [jax.ShapeDtypeStruct(a.shape, a.dtype) for a in passed],
        in_specs=[
            pl.BlockSpec((total, TILE), lambda t: (0, t)),
            pl.BlockSpec((total, hidden), lambda t: (0, 0)),
        ]
        + blocks,
        out_specs=[up_block] + blocks,
        compiler_params=pltpu.CompilerParams(vmem_limit_bytes=48 * 1024 * 1024),
    )(x_rows, dup_rows, *passed)


def expert_part(n, cap, route, queries, keys, values, stream, grad_out, gain, w_gate, w_up, w_down):
    frames, width = stream.shape
    hidden = w_gate.shape[1]
    total = n * 4 * cap
    bf, f32 = jnp.bfloat16, jnp.float32
    vmem = pl.BlockSpec(memory_space=pltpu.VMEM)
    hbm = pl.BlockSpec(memory_space=pl.ANY)
    dma = pltpu.SemaphoreType.DMA
    return pl.pallas_call(
        functools.partial(expert_kernel, n, cap),
        out_shape=(
            jax.ShapeDtypeStruct((frames, width), bf),
            jax.ShapeDtypeStruct((frames, width), bf),
            jax.ShapeDtypeStruct((frames, width), bf),
            jax.ShapeDtypeStruct((frames, width), bf),
            jax.ShapeDtypeStruct((width, hidden), f32),
            jax.ShapeDtypeStruct((hidden, width), f32),
            jax.ShapeDtypeStruct((n, 4, cap, width), bf),
            jax.ShapeDtypeStruct((total, hidden), bf),
        ),
        in_specs=[vmem] * 7 + [hbm] * 3,
        out_specs=(vmem,) * 4 + (hbm,) * 4,
        scratch_shapes=[
            pltpu.VMEM((n, cap, frames), bf),
            pltpu.VMEM((frames, width), bf),
            pltpu.VMEM((n, 2, cap, width), bf),
            pltpu.VMEM((2, 3, frames, width), bf),
            pltpu.VMEM((2, 2, frames, width), bf),
            pltpu.VMEM((2, 2, frames, width), bf),
            pltpu.VMEM((2, frames, width), f32),
            pltpu.VMEM((width // (2 * HEAD), 2 * frames, LEFT + frames), f32),
            pltpu.VMEM((n, 4, 2, cap, width), bf),
            pltpu.VMEM((width, hidden), bf),
            pltpu.VMEM((width, hidden), bf),
            pltpu.VMEM((hidden, width), bf),
            pltpu.VMEM((total, hidden), bf),
            pltpu.VMEM((total, hidden), bf),
            pltpu.VMEM((total, hidden), bf),
            pltpu.VMEM((n, 4, cap, width), bf),
            pltpu.VMEM((n, 2, cap, width), bf),
            pltpu.VMEM((n, cap, width), bf),
            pltpu.VMEM((n, cap, width), bf),
            pltpu.VMEM((2, width, hidden), f32),
            dma((3,)),
            dma((4,)),
            dma,
            dma((n, 4)),
            dma((n, 4)),
            dma((n, 2)),
            dma((n, 2)),
            dma((n,)),
            dma((n,)),
            dma((n,)),
            dma((n,)),
            dma((2, 3)),
            dma((2, 2)),
            dma((2,)),
            dma((2,)),
        ],
        compiler_params=pltpu.CompilerParams(
            collective_id=0, has_side_effects=True, vmem_limit_bytes=62 * 1024 * 1024
        ),
        cost_estimate=pl.CostEstimate(
            flops=16 * total * width * hidden, bytes_accessed=20 * width * hidden, transcendentals=0
        ),
    )(route, queries, keys, values, stream, grad_out, gain, w_gate, w_up, w_down)


def body(
    queries, keys, values, stream, grad_out, norm_gain, gate_probs, routes, w_gate, w_up, w_down
):
    frames = queries.shape[0]
    experts = lax.axis_size("tm")
    capacity = 3 * frames * routes.shape[1] // (2 * experts)
    cap = -(-capacity // 16) * 16
    route = jnp.concatenate([routes.astype(jnp.float32).T, gate_probs.T], 0)
    *passed, x_rows, dup_rows = expert_part(
        experts, cap, route, queries, keys, values, stream, grad_out, norm_gain[None, :],
        w_gate[0], w_up[0], w_down[0],
    )
    up_grad, grad_q, grad_k, grad_v, stream_grad, gate_grad, down_grad = finish(
        x_rows.reshape(-1, x_rows.shape[-1]), dup_rows, passed
    )
    return (
        grad_q, grad_k, grad_v, stream_grad, gate_grad[None], up_grad[None], down_grad[None]
    )


def solution(mesh):
    return jax.shard_map(
        body,
        mesh=mesh,
        in_specs=(
            P(("tm", "ep"), None),
            P(("tm", "ep"), None),
            P(("tm", "ep"), None),
            P(("tm", "ep"), None),
            P(("tm", "ep"), None),
            P(),
            P(("tm", "ep"), None),
            P(("tm", "ep"), None),
            P("tm", None, "ep"),
            P("tm", None, "ep"),
            P("tm", "ep", None),
        ),
        out_specs=(
            P(("tm", "ep"), None),
            P(("tm", "ep"), None),
            P(("tm", "ep"), None),
            P(("tm", "ep"), None),
            P("tm", None, "ep"),
            P("tm", None, "ep"),
            P("tm", "ep", None),
        ),
        check_vma=False,
    )
```

```python
import functools
import math

import jax
import jax.numpy as jnp
from jax import lax
from jax.experimental import pallas as pl
from jax.experimental.pallas import tpu as pltpu
from jax.sharding import PartitionSpec as P

D = 1024
HEADS = 16
HEAD = 64
SPAN = 64
LEFT = 256


EPSILON = 1e-06


MESH = pl.DeviceIdType.MESH
CHUNKS = 4
TILE = 256


def nt(a, b):
    return lax.dot_general(a, b, (((1,), (1,)), ((), ())), preferred_element_type=jnp.float32)


def tn(a, b):
    return lax.dot_general(a, b, (((0,), (0,)), ((), ())), preferred_element_type=jnp.float32)


def expert_kernel(
    n, cap,
    route_ref, q_ref, k_ref, v_ref, stream_ref, grad_ref, gain_ref, wg_hbm, wu_hbm, wd_hbm,
    gq_ref, gk_ref, gv_ref, sgrad_ref, gg_hbm, dg_hbm, x_hbm, dup_hbm,
    pick, norm_s, send, kv, halo_out, halo_in, own, kept, xg, wg, wu, wd, acted, dgate, dup, part, from_core, from_x, back, grads,
    w_sem, out_sem, loc_sem, d_send, d_recv, a_send, a_recv, b_send, b_recv, c_send, c_recv,
    kv_send, kv_recv, h_send, h_recv,
):
    i = lax.axis_index("tm")
    j = lax.axis_index("ep")
    j1 = j + 1 - 2 * (j % 2)
    j2 = (j + 2) % 4
    j3 = (j1 + 2) % 4
    width = stream_ref.shape[1]
    hidden = wg.shape[1]
    frames = stream_ref.shape[0]
    per = n // CHUNKS
    rows = per * 4 * cap

    weights = [
        pltpu.make_async_copy(src, dst, w_sem.at[q])
        for q, (src, dst) in enumerate(((wg_hbm, wg), (wu_hbm, wu), (wd_hbm, wd)))
    ]
    for copy in weights:
        copy.start()

    place = i * 4 + j
    places = n * 4

    def at(q):
        return (q // 4, q % 4)

    def nearby(act):
        for away in (1, 2):
            pl.when(place + away < places)(functools.partial(act, place + away))
            pl.when(place >= away)(functools.partial(act, place - away))

    barrier = pltpu.get_barrier_semaphore()
    nearby(lambda q: pl.semaphore_signal(barrier, inc=1, device_id=at(q), device_id_type=MESH))
    for d in range(1, n):
        pl.semaphore_signal(barrier, inc=1, device_id=((i + d) % n, j), device_id_type=MESH)
    pl.semaphore_signal(barrier, inc=1, device_id=(i, j1), device_id_type=MESH)
    pl.semaphore_signal(barrier, inc=1, device_id=(i, j2), device_id_type=MESH)

    stream_f = stream_ref[...].astype(jnp.float32)
    inverse_rms = lax.rsqrt(jnp.mean(stream_f * stream_f, -1, keepdims=True) + EPSILON)
    norm_s[...] = (stream_f * inverse_rms * gain_ref[...]).astype(jnp.bfloat16)

    kv[0, 2] = k_ref[...]
    kv[1, 2] = v_ref[...]

    names = lax.broadcasted_iota(jnp.int32, (n, frames), 0).astype(jnp.float32)
    chosen = [(names == route_ref[h : h + 1, :]).astype(jnp.float32) for h in range(2)]
    first = lax.broadcasted_iota(jnp.int32, (frames, frames), 0)
    second = lax.broadcasted_iota(jnp.int32, (frames, frames), 1)
    earlier = (first < second).astype(jnp.float32).astype(jnp.bfloat16)
    before = jnp.dot(
        (chosen[0] + chosen[1]).astype(jnp.bfloat16), earlier, preferred_element_type=jnp.float32
    )
    row_of = [
        route_ref[h : h + 1, :] * float(cap) + jnp.sum(before * chosen[h], 0, keepdims=True) for h in range(2)
    ]

    ahead = jnp.minimum(places - 1 - place, 2)
    pl.semaphore_wait(barrier, n + 1 + ahead + jnp.minimum(place, 2))

    def remote(src, dst, ssem, rsem, to):
        return pltpu.make_async_remote_copy(
            src_ref=src, dst_ref=dst, send_sem=ssem, recv_sem=rsem, device_id=to, device_id_type=MESH
        )

    def to_expert(d):
        return remote(send.at[d], xg.at[d, j], d_send.at[d, 0], d_recv.at[d, 0], ((i + d) % n, j))

    own_copy = pltpu.make_async_copy(send.at[0], xg.at[0, j], loc_sem)
    for d in list(range(1, n)) + [0]:
        e = (i + d) % n
        row_ids = (lax.broadcasted_iota(jnp.int32, (cap, frames), 0) + e * cap).astype(jnp.float32)
        hits = [(row_ids == row_of[h]).astype(jnp.float32) for h in range(2)]
        chance = sum(jnp.sum(hits[h] * route_ref[2 + h : 3 + h, :], 1, keepdims=True) for h in range(2))
        choice = (hits[0] + hits[1]).astype(jnp.bfloat16)
        pick[e] = choice
        send[d, 0] = jnp.dot(choice, norm_s[...], preferred_element_type=jnp.float32).astype(jnp.bfloat16)
        grad_rows = jnp.dot(choice, grad_ref[...], preferred_element_type=jnp.float32)
        send[d, 1] = (grad_rows * chance).astype(jnp.bfloat16)
        if d:
            to_expert(d).start()
        else:
            own_copy.start()

    even = j % 2 == 0

    def kv_all(away):
        return [
            remote(
                kv.at[q, 2], kv.at[q, 2 - away], kv_send.at[q, away], kv_recv.at[q, 2 - away], at(place + away)
            )
            for q in range(2)
        ]

    def kv_forwards():
        return [
            remote(kv.at[q, 1], kv.at[q, 0], kv_send.at[q, 0], kv_recv.at[q, 0], at(place + 1))
            for q in range(2)
        ]

    def each(copies, what):
        for copy in copies:
            getattr(copy, what)()

    has_next = place + 1 < places
    has_second = place + 2 < places

    @pl.when(has_next)
    def _():
        each(kv_all(1), "start")

    @pl.when(jnp.logical_and(even, has_second))
    def _():
        each(kv_all(2), "start")

    def kv_forward():
        @pl.when(place >= 1)
        def _():
            each(kv_all(1), "wait_recv")

        @pl.when(place < 1)
        def _():
            kv[:, 1] = jnp.zeros_like(kv[:, 1])

        @pl.when(jnp.logical_and(even, place >= 1))
        def _():
            each(kv_forwards(), "start")

    def kv_finish():
        @pl.when(place >= 2)
        def _():
            each(kv_all(2), "wait_recv")

        @pl.when(place < 2)
        def _():
            kv[:, 0] = jnp.zeros_like(kv[:, 0])

    scale = 1.0 / math.sqrt(HEAD)
    lane = lax.broadcasted_iota(jnp.int32, (1, 2 * HEAD), 1)
    low = (lane < HEAD).astype(jnp.float32).astype(jnp.bfloat16)
    high = (lane >= HEAD).astype(jnp.float32).astype(jnp.bfloat16)
    reach = LEFT + frames

    def paired(block):
        return jnp.concatenate([block * low, block * high], 0)

    def pair_columns(t):
        return pl.ds(pl.multiple_of(t * 2 * HEAD, 2 * HEAD), 2 * HEAD)

    def attend(begin, stop):
        row = lax.broadcasted_iota(jnp.int32, (2 * frames, reach), 0)
        col = lax.broadcasted_iota(jnp.int32, (2 * frames, reach), 1)
        start = (row % frames) // SPAN * SPAN
        seen = jnp.logical_and(col >= start, col < start + SPAN + LEFT)
        seen = jnp.logical_and(seen, col >= LEFT - place * frames)

        @pl.loop(begin, stop, unroll=2)
        def _(t):
            cols = pair_columns(t)
            keys = kv[0, :, :, cols].reshape(reach, 2 * HEAD)
            scores = nt(paired(q_ref[:, cols]), keys) * scale
            scores = jnp.where(seen, scores, -jnp.inf)
            exps = jnp.exp(scores - jnp.max(scores, -1, keepdims=True))
            probs = exps / jnp.sum(exps, -1, keepdims=True)
            kept[t] = probs

    def attend_back(half):
        begin = half * (width // (4 * HEAD))

        @pl.loop(begin, begin + width // (4 * HEAD), unroll=2)
        def _(t):
            cols = pair_columns(t)
            half_cols = pair_columns(t - begin)
            keys = kv[0, :, :, cols].reshape(reach, 2 * HEAD)
            vals = kv[1, :, :, cols].reshape(reach, 2 * HEAD)
            probs = kept[t]
            pround = probs.astype(jnp.bfloat16)
            outs = paired(sgrad_ref[:, cols])
            dprob = nt(outs, vals)
            row_delta = jnp.sum(pround.astype(jnp.float32) * dprob, -1, keepdims=True)
            dscore = (probs * (dprob - row_delta)).astype(jnp.bfloat16)
            gq = jnp.dot(dscore, keys, preferred_element_type=jnp.float32) * scale
            gq_ref[:, cols] = jnp.where(lane < HEAD, gq[:frames], gq[frames:]).astype(jnp.bfloat16)
            for q, total in ((0, tn(dscore, paired(q_ref[:, cols])) * scale), (1, tn(pround, outs))):
                for piece in range(2):
                    part_rows = total[piece * frames : (piece + 1) * frames]
                    halo_out[half, piece, q, :, half_cols] = part_rows.astype(jnp.bfloat16)
                own[q, :, cols] = total[LEFT:]

    def halo_copy(half, away):
        return remote(
            halo_out.at[half, 2 - away],
            halo_in.at[half, 2 - away],
            h_send.at[half, away - 1],
            h_recv.at[half, away - 1],
            at(place - away),
        )

    def own_to_core(d):
        return remote(xg.at[d, j], xg.at[d, j], d_send.at[d, 1], d_recv.at[d, 1], (i, j1))

    def own_to_x(d):
        return remote(xg.at[d, j], xg.at[d, j], d_send.at[d, 2], d_recv.at[d, 2], (i, j2))

    def x_to_core(d):
        return remote(xg.at[d, j2], xg.at[d, j2], d_send.at[d, 3], d_recv.at[d, 3], (i, j1))

    def span(c):
        return range(c * per, (c + 1) * per)

    def forward_own(c):
        for d in span(c):
            if d:
                to_expert(d).wait_recv()
            else:
                own_copy.wait()
            own_to_x(d).start()
            own_to_core(d).start()

    def forward_x(c):
        for d in span(c):
            own_to_x(d).wait_recv()
            x_to_core(d).start()

    def gather(c):
        for d in span(c):
            own_to_core(d).wait_recv()
            x_to_core(d).wait_recv()

    def compute(c):
        here = pl.ds(c * rows, rows)

        @pl.loop(0, hidden // TILE)
        def _(t):
            cols = pl.ds(pl.multiple_of(t * TILE, TILE), TILE)
            x = xg[c * per : (c + 1) * per, :, 0].reshape(rows, width)
            g = xg[c * per : (c + 1) * per, :, 1].reshape(rows, width)
            gate_pre = jnp.dot(x, wg[:, cols], preferred_element_type=jnp.float32)
            up_pre = jnp.dot(x, wu[:, cols], preferred_element_type=jnp.float32)
            dact = nt(g, wd[cols, :])
            sig = jax.nn.sigmoid(gate_pre)
            silu = gate_pre * sig
            acted[here, cols] = (silu * up_pre).astype(jnp.bfloat16)
            dgate[here, cols] = (dact * up_pre * sig * (1.0 + gate_pre * (1.0 - sig))).astype(jnp.bfloat16)
            dup[here, cols] = (dact * silu).astype(jnp.bfloat16)

        @pl.loop(0, width // TILE)
        def _(t):
            cols = pl.ds(pl.multiple_of(t * TILE, TILE), TILE)
            dx = nt(dgate[here, :], wg[cols, :]) + nt(dup[here, :], wu[cols, :])
            part[c * per : (c + 1) * per, :, :, cols] = dx.astype(jnp.bfloat16).reshape(per, 4, cap, TILE)

    def core_copies(d):
        return (
            remote(part.at[d, j1], from_core.at[d, 0], a_send.at[d, 0], a_recv.at[d, 0], (i, j1)),
            remote(part.at[d, j3], from_core.at[d, 1], a_send.at[d, 1], a_recv.at[d, 1], (i, j1)),
        )

    def x_copy(d):
        return remote(part.at[d, j2], from_x.at[d], b_send.at[d], b_recv.at[d], (i, j2))

    def home_copy(d):
        return remote(part.at[d, j], back.at[i], c_send.at[d], c_recv.at[d], ((i + n - d) % n, j))

    def stage_a(c):
        for d in span(c):
            for copy in core_copies(d):
                copy.start()

    def stage_b(c):
        for d in span(c):
            core_copies(d)[1].wait_recv()
            total = part[d, j2].astype(jnp.float32) + from_core[d, 1].astype(jnp.float32)
            part[d, j2] = total.astype(jnp.bfloat16)
            x_copy(d).start()

    def stage_c(c):
        for d in span(c):
            core_copies(d)[0].wait_recv()
            x_copy(d).wait_recv()
            total = part[d, j].astype(jnp.float32) + from_core[d, 0].astype(jnp.float32)
            total = (total + from_x[d].astype(jnp.float32)).astype(jnp.bfloat16)
            if d:
                part[d, j] = total
                home_copy(d).start()
            else:
                back[i] = total

    pairs = width // (2 * HEAD)
    forward_own(0)
    each(weights, "wait")
    forward_own(1)
    for c in range(CHUNKS):
        forward_x(c)
        gather(c)
        compute(c)
        stage_a(c)
        if c + 2 < CHUNKS:
            forward_own(c + 2)
        if c >= 1:
            stage_b(c - 1)
        if c >= 2:
            stage_c(c - 2)
        if c == 1:
            kv_forward()
    kv_finish()
    attend(0, pairs // 2)
    stage_b(CHUNKS - 1)
    stage_c(CHUNKS - 2)
    attend(pairs // 2, pairs)
    stage_c(CHUNKS - 1)

    total_rows = n * 4 * cap
    writes = [
        pltpu.make_async_copy(grads.at[0], dg_hbm, out_sem.at[0]),
        pltpu.make_async_copy(grads.at[1], gg_hbm, out_sem.at[1]),
        pltpu.make_async_copy(xg.at[:, :, 0], x_hbm, out_sem.at[2]),
        pltpu.make_async_copy(dup, dup_hbm, out_sem.at[3]),
    ]
    writes[2].start()
    writes[3].start()

    def down_grads(begin, stop):
        @pl.loop(begin, stop)
        def _(t):
            cols = pl.ds(pl.multiple_of(t * TILE, TILE), TILE)
            lhs = acted[:, cols]
            for q in range(0, width, 512):
                rhs = xg[:, :, 1, :, q : q + 512].reshape(total_rows, 512)
                grads[0, cols, q : q + 512] = tn(lhs, rhs)

    def gate_grads(begin, stop):
        @pl.loop(begin, stop)
        def _(t):
            cols = pl.ds(pl.multiple_of(t * TILE, TILE), TILE)
            lhs = xg[:, :, 0, :, cols].reshape(total_rows, TILE)
            for q in range(0, hidden, 512):
                grads[1, cols, q : q + 512] = tn(lhs, dgate[:, q : q + 512])

    down_tiles = hidden // TILE
    gate_tiles = width // TILE
    down_grads(0, down_tiles)
    writes[0].start()

    for d in range(1, n):
        home_copy(d).wait_recv()
    dnormed = tn(pick[...].reshape(n * cap, frames), back[...].reshape(n * cap, width))
    stream_f = stream_ref[...].astype(jnp.float32)
    inverse_rms = lax.rsqrt(jnp.mean(stream_f * stream_f, -1, keepdims=True) + EPSILON)
    scaled = stream_f * inverse_rms
    weighted = dnormed * gain_ref[...]
    dstream = inverse_rms * (weighted - scaled * jnp.mean(weighted * scaled, -1, keepdims=True))
    sgrad_ref[...] = (grad_ref[...].astype(jnp.float32) + dstream).astype(jnp.bfloat16)

    for half in range(2):
        attend_back(half)
        for away in (1, 2):
            @pl.when(place >= away)
            def _():
                halo_copy(half, away).start()

    gate_grads(0, gate_tiles)
    writes[1].start()

    wide = width // 2
    for half in range(2):
        for away in (1, 2):
            @pl.when(place + away < places)
            def _():
                halo_copy(half, away).wait_recv()

            @pl.when(place + away >= places)
            def _():
                halo_in[half, 2 - away] = jnp.zeros_like(halo_in[half, 2 - away])

        for q, out_ref in ((0, gk_ref), (1, gv_ref)):
            cols = slice(half * wide, (half + 1) * wide)
            total = own[q, :, cols] + halo_in[half, 0, q].astype(jnp.float32)
            total = total + halo_in[half, 1, q].astype(jnp.float32)
            out_ref[:, cols] = total.astype(jnp.bfloat16)

    for half in range(2):
        for away in (1, 2):
            @pl.when(place >= away)
            def _():
                halo_copy(half, away).wait_send()

    @pl.when(has_next)
    def _():
        each(kv_all(1), "wait_send")

    @pl.when(jnp.logical_and(even, has_second))
    def _():
        each(kv_all(2), "wait_send")

    @pl.when(jnp.logical_and(even, place >= 1))
    def _():
        each(kv_forwards(), "wait_send")

    for d in range(n):
        if d:
            to_expert(d).wait_send()
            home_copy(d).wait_send()
        own_to_core(d).wait_send()
        own_to_x(d).wait_send()
        x_to_core(d).wait_send()
        for copy in core_copies(d):
            copy.wait_send()
        x_copy(d).wait_send()
    each(writes, "wait")


def finish_kernel(x_ref, dup_ref, *refs):
    half = len(refs) // 2
    refs[half][...] = tn(x_ref[...], dup_ref[...])
    for src, dst in zip(refs[:half], refs[half + 1 :]):
        dst[...] = src[...]


def finish(x_rows, dup_rows, passed):
    total, width = x_rows.shape
    hidden = dup_rows.shape[1]
    steps = width // TILE
    blocks = [pl.BlockSpec((a.shape[0] // steps, a.shape[1]), lambda t: (t, 0)) for a in passed]
    up_block = pl.BlockSpec((TILE, hidden), lambda t: (t, 0))
    return pl.pallas_call(
        finish_kernel,
        grid=(steps,),
        out_shape=[jax.ShapeDtypeStruct((width, hidden), jnp.float32)]
        + [jax.ShapeDtypeStruct(a.shape, a.dtype) for a in passed],
        in_specs=[
            pl.BlockSpec((total, TILE), lambda t: (0, t)),
            pl.BlockSpec((total, hidden), lambda t: (0, 0)),
        ]
        + blocks,
        out_specs=[up_block] + blocks,
        compiler_params=pltpu.CompilerParams(vmem_limit_bytes=62 * 1024 * 1024),
    )(x_rows, dup_rows, *passed)


def expert_part(n, cap, route, queries, keys, values, stream, grad_out, gain, w_gate, w_up, w_down):
    frames, width = stream.shape
    hidden = w_gate.shape[1]
    total = n * 4 * cap
    bf, f32 = jnp.bfloat16, jnp.float32
    vmem = pl.BlockSpec(memory_space=pltpu.VMEM)
    hbm = pl.BlockSpec(memory_space=pl.ANY)
    dma = pltpu.SemaphoreType.DMA
    return pl.pallas_call(
        functools.partial(expert_kernel, n, cap),
        out_shape=(
            jax.ShapeDtypeStruct((frames, width), bf),
            jax.ShapeDtypeStruct((frames, width), bf),
            jax.ShapeDtypeStruct((frames, width), bf),
            jax.ShapeDtypeStruct((frames, width), bf),
            jax.ShapeDtypeStruct((width, hidden), f32),
            jax.ShapeDtypeStruct((hidden, width), f32),
            jax.ShapeDtypeStruct((n, 4, cap, width), bf),
            jax.ShapeDtypeStruct((total, hidden), bf),
        ),
        in_specs=[vmem] * 7 + [hbm] * 3,
        out_specs=(vmem,) * 4 + (hbm,) * 4,
        scratch_shapes=[
            pltpu.VMEM((n, cap, frames), bf),
            pltpu.VMEM((frames, width), bf),
            pltpu.VMEM((n, 2, cap, width), bf),
            pltpu.VMEM((2, 3, frames, width), bf),
            pltpu.VMEM((2, 2, 2, frames, width // 2), bf),
            pltpu.VMEM((2, 2, 2, frames, width // 2), bf),
            pltpu.VMEM((2, frames, width), f32),
            pltpu.VMEM((width // (2 * HEAD), 2 * frames, LEFT + frames), f32),
            pltpu.VMEM((n, 4, 2, cap, width), bf),
            pltpu.VMEM((width, hidden), bf),
            pltpu.VMEM((width, hidden), bf),
            pltpu.VMEM((hidden, width), bf),
            pltpu.VMEM((total, hidden), bf),
            pltpu.VMEM((total, hidden), bf),
            pltpu.VMEM((total, hidden), bf),
            pltpu.VMEM((n, 4, cap, width), bf),
            pltpu.VMEM((n, 2, cap, width), bf),
            pltpu.VMEM((n, cap, width), bf),
            pltpu.VMEM((n, cap, width), bf),
            pltpu.VMEM((2, width, hidden), f32),
            dma((3,)),
            dma((4,)),
            dma,
            dma((n, 4)),
            dma((n, 4)),
            dma((n, 2)),
            dma((n, 2)),
            dma((n,)),
            dma((n,)),
            dma((n,)),
            dma((n,)),
            dma((2, 3)),
            dma((2, 2)),
            dma((2, 2)),
            dma((2, 2)),
        ],
        compiler_params=pltpu.CompilerParams(
            collective_id=0, has_side_effects=True, vmem_limit_bytes=62 * 1024 * 1024
        ),
        cost_estimate=pl.CostEstimate(
            flops=16 * total * width * hidden, bytes_accessed=20 * width * hidden, transcendentals=0
        ),
    )(route, queries, keys, values, stream, grad_out, gain, w_gate, w_up, w_down)


def body(
    queries, keys, values, stream, grad_out, norm_gain, gate_probs, routes, w_gate, w_up, w_down
):
    frames = queries.shape[0]
    experts = lax.axis_size("tm")
    capacity = 3 * frames * routes.shape[1] // (2 * experts)
    cap = -(-capacity // 16) * 16
    route = jnp.concatenate([routes.astype(jnp.float32).T, gate_probs.T], 0)
    *passed, x_rows, dup_rows = expert_part(
        experts, cap, route, queries, keys, values, stream, grad_out, norm_gain[None, :],
        w_gate[0], w_up[0], w_down[0],
    )
    up_grad, grad_q, grad_k, grad_v, stream_grad, gate_grad, down_grad = finish(
        x_rows.reshape(-1, x_rows.shape[-1]), dup_rows, passed
    )
    return (
        grad_q, grad_k, grad_v, stream_grad, gate_grad[None], up_grad[None], down_grad[None]
    )


def solution(mesh):
    return jax.shard_map(
        body,
        mesh=mesh,
        in_specs=(
            P(("tm", "ep"), None),
            P(("tm", "ep"), None),
            P(("tm", "ep"), None),
            P(("tm", "ep"), None),
            P(("tm", "ep"), None),
            P(),
            P(("tm", "ep"), None),
            P(("tm", "ep"), None),
            P("tm", None, "ep"),
            P("tm", None, "ep"),
            P("tm", "ep", None),
        ),
        out_specs=(
            P(("tm", "ep"), None),
            P(("tm", "ep"), None),
            P(("tm", "ep"), None),
            P(("tm", "ep"), None),
            P("tm", None, "ep"),
            P("tm", None, "ep"),
            P("tm", "ep", None),
        ),
        check_vma=False,
    )
```
